512 devices in a mesh: space: 32 (over z, y_lo), filt: 16 (over y_hi, x, core).
Axes of the slice: x: 4, y: 4 (y_hi: 2, y_lo: 2; y = y_hi * 2 + y_lo), z: 16, core: 2. Of those that a mesh axis runs over, the one named last changes fastest.
Arguments:
- volume: bfloat16 [32, 256, 2, 128], P('space', 'filt'), may hold values from -6 to 6
- first_weight: bfloat16 [128, 64, 256], P('filt'), may hold values from -0.125 to 0.125
- first_bias: bfloat16 [128], P('filt'), may hold values from -3 to 3
- second_weight: bfloat16 [128, 27, 128], P('filt'), may hold values from -0.109375 to 0.109375
- second_bias: bfloat16 [128], P('filt'), may hold values from -3 to 3
- cotangent: bfloat16 [64, 128, 4, 256], P('space', 'filt'), may hold values from -6 to 6
Outputs:
- result: bfloat16 [64, 128, 4, 256], P('space', 'filt')
- grad_volume: bfloat16 [32, 256, 2, 128], P('space', 'filt')
- grad_first: float32 [128, 64, 256], P('filt')
- grad_first_bias: float32 [128], P('filt')
- grad_second: float32 [128, 27, 128], P('filt')
- grad_second_bias: float32 [128], P('filt')
The draws below stay inside these ranges and needn't reach their ends.
All inputs are finite; a program needn't handle non-finite values.
Results may differ from the reference program's by a relative error of at most 0.0085.
Values may be sent and summed in bfloat16 or wider, within the bound.
No kernel may reach another device: no remote copies, remote signals or barrier semaphores. Data moves between devices by JAX's collectives and lax.ppermute only.
A program may use at most 64 MiB of HBM per device.

```python
import math
import jax
import jax.numpy as jnp
from jax import lax

CIN = 256
CMID = 128
COUT = 128
XI = 2
YI = 128
ZI = 32
ZO = 64
XO = 4
YO = 256
CELLS = 65536


def steps_of(stream_key, extent, shards, low, high):
    factor_of = 1.0
    for position, blocks in shards:
        steps = jax.random.uniform(jax.random.fold_in(jax.random.fold_in(stream_key, 6), position), (blocks,), jnp.float32, low / len(shards), high / len(shards))
        factor_of = factor_of * jnp.repeat(jnp.exp(steps), extent[position] // blocks).reshape((-1,) + (1,) * (len(extent) - 1 - position))
    return factor_of


def gaussian(key, dims, width, bound, cuts=(), kind=jnp.bfloat16):
    array = width * jax.random.normal(key, dims, jnp.float32)
    if cuts:
        array = array * steps_of(key, dims, cuts, -0.22, 0.18)
    return jnp.clip(array, -bound, bound).astype(kind)


def setup_inputs(seed: int = 0) -> dict:
    seeds = jax.random.split(jax.random.key(seed), 7)
    return {
        "volume": gaussian(seeds[0], (ZI, CIN, XI, YI), 1.0, 6.0, ((0, 32), (1, 16))),
        "first_weight": gaussian(seeds[1], (CMID, 64, CIN), (8 * CIN) ** -0.5, 0.125, ((0, 16),)),
        "first_bias": gaussian(seeds[2], (CMID,), 0.5, 3.0, ((0, 16),)),
        "second_weight": gaussian(seeds[3], (COUT, 27, CMID), (27 * CMID) ** -0.5, 0.109375, ((0, 16),)),
        "second_bias": gaussian(seeds[4], (COUT,), 0.5, 3.0, ((0, 16),)),
        "cotangent": gaussian(seeds[5], (ZO, COUT, XO, YO), 1.0, 6.0, ((0, 32), (1, 16))),
    }


TAP_PLACE = ((1, 1), (0, 0), (1, 0), (0, -1))

def moved(field, along_z, along_x, along_y):
    return jnp.roll(field, (-along_z, -along_x, -along_y), axis=(0, 2, 3))

def alternate(parts):
    stacked = jnp.stack(parts)
    planes, channels, extent_x, extent_y = stacked.shape[1:]
    stacked = stacked.reshape(2, 2, 2, planes, channels, extent_x, extent_y)
    return stacked.transpose(3, 0, 4, 5, 1, 6, 2).reshape(2 * planes, channels, 2 * extent_x, 2 * extent_y)

def upsample(source, weight):
    parts = {}
    for tap_z in range(4):
        parity_z, offset_z = TAP_PLACE[tap_z]
        for tap_x in range(4):
            parity_x, offset_x = TAP_PLACE[tap_x]
            for tap_y in range(4):
                parity_y, offset_y = TAP_PLACE[tap_y]
                term = jnp.einsum('dc,zcxy->zdxy', weight[:, tap_z * 16 + tap_x * 4 + tap_y, :], moved(source, offset_z, offset_x, offset_y))
                place = (parity_z, parity_x, parity_y)
                parts[place] = parts[place] + term if place in parts else term
    return alternate([parts[first, second, third] for first in range(2) for second in range(2) for third in range(2)])

def reference(volume, first_weight, first_bias, second_weight, second_bias, cotangent):
    source = volume.astype(jnp.float32)
    weight_one = first_weight.astype(jnp.float32)
    weight_two = second_weight.astype(jnp.float32)
    lifted = upsample(source, weight_one) + first_bias.astype(jnp.float32)[None, :, None, None]
    hidden = lifted.astype(jnp.bfloat16).astype(jnp.float32)
    taps = [(shift_z, shift_x, shift_y) for shift_z in (-1, 0, 1) for shift_x in (-1, 0, 1) for shift_y in (-1, 0, 1)]
    pre = jnp.zeros((hidden.shape[0], weight_two.shape[0], hidden.shape[2], hidden.shape[3]), jnp.float32)
    for index, (shift_z, shift_x, shift_y) in enumerate(taps):
        pre = pre + jnp.einsum('dc,zcxy->zdxy', weight_two[:, index, :], moved(hidden, shift_z, shift_x, shift_y))
    pre = pre + second_bias.astype(jnp.float32)[None, :, None, None]
    sigma = jax.nn.sigmoid(pre)
    result = (pre * sigma).astype(jnp.bfloat16)
    dpre = (cotangent.astype(jnp.float32) * sigma * (1.0 + pre * (1.0 - sigma))).astype(jnp.bfloat16).astype(jnp.float32)
    second_terms = []
    dhidden = jnp.zeros_like(hidden)
    for index, (shift_z, shift_x, shift_y) in enumerate(taps):
        second_terms.append(jnp.einsum('zdxy,zcxy->dc', dpre, moved(hidden, shift_z, shift_x, shift_y)))
        dhidden = dhidden + jnp.einsum('dc,zdxy->zcxy', weight_two[:, index, :], moved(dpre, -shift_z, -shift_x, -shift_y))
    raw_second = jnp.stack(second_terms, axis=1)
    raw_second_bias = lax.optimization_barrier(jnp.sum(dpre, axis=(0, 2, 3)))
    dhidden = dhidden.astype(jnp.bfloat16).astype(jnp.float32)
    first_terms = []
    grad_volume = jnp.zeros_like(source)
    for tap_z in range(4):
        for tap_x in range(4):
            for tap_y in range(4):
                columns = jnp.roll(dhidden, (1 - tap_z, 1 - tap_x, 1 - tap_y), axis=(0, 2, 3))[::2, :, ::2, ::2]
                first_terms.append(jnp.einsum('zdxy,zcxy->dc', columns, source))
                grad_volume = grad_volume + jnp.einsum('dc,zdxy->zcxy', weight_one[:, tap_z * 16 + tap_x * 4 + tap_y, :], columns)
    raw_first = jnp.stack(first_terms, axis=1)
    raw_first_bias = lax.optimization_barrier(jnp.sum(dhidden, axis=(0, 2, 3)))
    scale = 1.0 / math.sqrt(CELLS)
    return (result, grad_volume.astype(jnp.bfloat16), raw_first * scale, raw_first_bias * scale, raw_second * scale, raw_second_bias * scale)
```

```python
import math

import jax
import jax.numpy as jnp
from jax import lax
from jax.experimental import pallas as pl
from jax.experimental.pallas import tpu as pltpu
from jax.sharding import PartitionSpec as P

F32 = jnp.float32
BF16 = jnp.bfloat16
TAP_PLACE = ((1, 1), (0, 0), (1, 0), (0, -1))
LANE = 128
PLANE = 1024
NEAR = 8


def vmem_call(body, outs, scratch=(), limit=24 * 1024 * 1024):
    return pl.pallas_call(
        body,
        out_shape=outs,
        scratch_shapes=list(scratch),
        compiler_params=pltpu.CompilerParams(vmem_limit_bytes=limit),
    )


def ahead(value, step):
    extent = value.shape[-1]
    return value if step == 0 else pltpu.roll(value, (-step) % extent, value.ndim - 1)


def dot(a, b, dims=((1,), (0,))):
    return lax.dot_general(a, b, (dims, ((), ())), preferred_element_type=F32)


def hidden_kernel(weight, source, bias, out, taps):
    taps[...] = dot(weight[...], source[...])

    def tap(kz, kx, ky, plane, xi):
        row = (kz * 16 + kx * 4 + ky) * 8
        col = plane * 256 + xi * LANE
        return taps[row : row + 8, col : col + LANE]

    for plane in range(4):
        parity_z = (plane + 1) % 2
        base_z = (plane + 1) // 2
        along_z = [(k, base_z + off) for k, (par, off) in enumerate(TAP_PLACE) if par == parity_z]
        for x in range(4):
            along_x = [
                (k, (x // 2 + off) % 2) for k, (par, off) in enumerate(TAP_PLACE) if par == x % 2
            ]
            for parity_y in range(2):
                total = bias[...]
                for ky, (par, off) in enumerate(TAP_PLACE):
                    if par != parity_y:
                        continue
                    part = None
                    for kz, iz in along_z:
                        for kx, ix in along_x:
                            term = tap(kz, kx, ky, iz, ix)
                            part = term if part is None else part + term
                    total = total + ahead(part, off)
                col = plane * PLANE + x * 256 + parity_y * LANE
                out[:, col : col + LANE] = total.astype(BF16)


def spread_rows(rows, cols):
    natural = lax.broadcasted_iota(jnp.int32, (rows, cols), 0)
    split = lax.broadcasted_iota(jnp.int32, (rows, cols), 1)
    return jnp.where(natural == 2 * (split % LANE) + split // LANE, 1.0, 0.0).astype(BF16)


def split_kernel(field, out, rows):
    rows[...] = dot(field[...], spread_rows(256, 256))
    for z in range(2):
        for x in range(4):
            col = z * PLANE + x * 256
            for e in range(8):
                line = z * 32 + e * 4 + x
                out[e : e + 1, col : col + 256] = rows[line : line + 1, :]


def activate_kernel(hidden, weight, bias, cot, result, dpre, taps, rows):
    taps[...] = dot(weight[...], hidden[...])

    def column(plane, x, parity):
        return plane * PLANE + (x % 4) * 256 + parity * LANE

    for z in range(2):
        for x in range(4):
            halves = []
            for parity in range(2):
                pre = bias[...]
                for ty in (-1, 0, 1):
                    other = (parity + ty) % 2
                    step = (parity + ty) // 2
                    part = None
                    for tz in range(3):
                        for tx in range(3):
                            row = (tz * 9 + tx * 3 + ty + 1) * 8
                            col = column(z + tz, x + tx - 1, other)
                            term = taps[row : row + 8, col : col + LANE]
                            part = term if part is None else part + term
                    pre = pre + ahead(part, step)
                sigma = 1.0 / (1.0 + jnp.exp(-pre))
                halves.append((pre * sigma).astype(BF16))
                col = column(z, x, parity)
                slope = cot[:, col : col + LANE] * sigma * (1.0 + pre * (1.0 - sigma))
                dpre[:, col : col + LANE] = slope.astype(BF16)
            both = jnp.concatenate(halves, axis=1)
            natural = dot(both, spread_rows(256, 256), ((1,), (1,)))
            for e in range(8):
                line = z * 32 + e * 4 + x
                rows[line : line + 1, :] = natural[e : e + 1, :]
    result[...] = rows[...].astype(BF16)


def mix_back_kernel(low, dpre, high, hidden, weight, share, raw, cols, colb):
    planes = (
        low[...].astype(F32),
        dpre[:, :PLANE].astype(F32),
        dpre[:, PLANE:].astype(F32),
        high[...].astype(F32),
    )

    def cells(plane, x, parity):
        col = (x % 4) * 256 + parity * LANE
        return planes[plane][:, col : col + LANE]

    for z in range(2):
        for tz in range(3):
            for x in range(4):
                for parity in range(2):
                    for ty in (-1, 0, 1):
                        other = (parity - ty) % 2
                        step = (parity - ty) // 2
                        for tx in range(3):
                            value = ahead(cells(z + 2 - tz, x - (tx - 1), other), step)
                            row = (tz * 9 + tx * 3 + ty + 1) * 8
                            col = z * PLANE + x * 256 + parity * LANE
                            cols[row : row + 8, col : col + LANE] = value
    cols[216:256, :] = jnp.zeros((40, 2 * PLANE), F32)
    colb[...] = cols[...].astype(BF16)
    share[...] = dot(weight[...], colb[...]).astype(BF16)
    raw[...] = dot(colb[...], hidden[...], ((1,), (1,)))
    total = jnp.sum(planes[1] + planes[2], axis=1, keepdims=True)
    raw[216:224, :] = jnp.broadcast_to(total, (8, LANE))


def pick_columns(field, out, base):
    for kx in range(4):
        for ky in range(4):
            parity, step = (ky - 1) % 2, (ky - 1) // 2
            for xi in range(2):
                x = (2 * xi - 1 + kx) % 4
                col = x * 256 + parity * LANE
                row = base + (kx * 4 + ky) * 8
                out[row : row + 8, xi * LANE : (xi + 1) * LANE] = ahead(
                    field[:, col : col + LANE], step
                )


def lift_back_kernel(parts, source, raw_second, dhidden, message, cols, raw, second):
    total = parts[0].astype(F32)
    for f in range(1, 16):
        total = total + parts[f].astype(F32)
    rounded = total.astype(BF16)
    dhidden[...] = rounded
    total = rounded.astype(F32)
    pick_columns(total[:, :PLANE], cols, 0)
    pick_columns(total[:, PLANE:], cols, LANE)
    for kz, (plane, place) in enumerate(((1, 2), (0, 1), (1, 1), (0, 0))):
        raw[kz * LANE : (kz + 1) * LANE, :] = dot(
            cols[plane * LANE : (plane + 1) * LANE, :].astype(BF16),
            source[:, place * 256 : (place + 1) * 256],
            ((1,), (1,)),
        )
    second[...] = raw_second[...]
    sums = (second[216:224, :], jnp.broadcast_to(jnp.sum(total, axis=1, keepdims=True), (8, LANE)))
    for i, value in enumerate(sums):
        high = value.astype(BF16).astype(F32)
        second[216 + 16 * i : 224 + 16 * i, :] = high
        second[224 + 16 * i : 232 + 16 * i, :] = value - high
    for i in range(NEAR):
        block = raw[64 * i : 64 * (i + 1), :].astype(BF16)
        message[i, 0:64, :] = block[:, :LANE]
        message[i, 64:128, :] = block[:, LANE:]
        message[i, 128:160, :] = second[32 * i : 32 * (i + 1), :].astype(BF16)


def lift_input_kernel(low, dhidden, high, weight, share, cols):
    own = dhidden[...].astype(F32)
    pick_columns(low[...].astype(F32), cols, 0)
    pick_columns(own[:, :PLANE], cols, LANE)
    pick_columns(own[:, PLANE:], cols, 2 * LANE)
    pick_columns(high[...].astype(F32), cols, 3 * LANE)
    share[...] = dot(weight[...], cols[...].astype(BF16)).astype(BF16)


def sum_kernel(parts, out):
    total = parts[0].astype(F32)
    for i in range(1, parts.shape[0]):
        total = total + parts[i].astype(F32)
    out[...] = total.astype(out.dtype)


def finish_kernel(scale, parts, first, second, bias, left, right, rest):
    for i in range(NEAR):
        left[64 * i : 64 * (i + 1), :] = parts[i, 0:64, :].astype(F32) * scale
        right[64 * i : 64 * (i + 1), :] = parts[i, 64:128, :].astype(F32) * scale
        rest[32 * i : 32 * (i + 1), :] = parts[i, 128:160, :].astype(F32) * scale
    for d in range(8):
        first[d, :, :LANE] = left[pl.ds(d, 64, stride=8), :]
        first[d, :, LANE:] = right[pl.ds(d, 64, stride=8), :]
    second[...] = rest[0:216, :]
    bias[0:8, :] = rest[216:224, :] + rest[224:232, :]
    bias[8:16, :] = rest[232:240, :] + rest[240:248, :]


def shifted(value, step):
    count = lax.axis_size("space")
    return lax.ppermute(value, "space", [(i, (i + step) % count) for i in range(count)])


def gathered(value):
    copies = jnp.broadcast_to(value[None], (lax.axis_size("filt"),) + value.shape)
    return lax.all_to_all(copies, "filt", 0, 0, tiled=True)


def near_exchange(value):
    count = lax.axis_size("space")
    groups = [[g + i for i in range(NEAR)] for g in range(0, count, NEAR)]
    return lax.all_to_all(value, "space", 0, 0, axis_index_groups=groups, tiled=True)


def per_device(volume, first_weight, first_bias, second_weight, second_bias, cotangent):
    struct = jax.ShapeDtypeStruct
    wide = lambda bias: jnp.broadcast_to(bias.astype(F32)[:, None], (8, LANE))
    first_rows = first_weight.transpose(1, 0, 2).reshape(512, 256)
    first_turned = first_weight.transpose(2, 1, 0).reshape(256, 512)
    second_rows = second_weight.transpose(1, 0, 2).reshape(216, LANE)
    second_rows = jnp.pad(second_rows, ((0, 8), (0, 0)))
    second_turned = jnp.pad(second_weight.transpose(2, 1, 0).reshape(LANE, 216), ((0, 0), (0, 40)))

    own = volume.reshape(16, 256)
    source = jnp.concatenate([shifted(own, 1), own, shifted(own, -1)], axis=1)
    source = gathered(source).reshape(256, 768)
    cot = vmem_call(
        split_kernel, struct((8, 2 * PLANE), F32), [pltpu.VMEM((64, 256), F32)]
    )(cotangent.reshape(64, 256))
    hidden = vmem_call(
        hidden_kernel, struct((8, 4 * PLANE), BF16), [pltpu.VMEM((512, 768), F32)]
    )(first_rows, source, wide(first_bias))
    hidden = gathered(hidden).reshape(LANE, 4 * PLANE)

    result, dpre = vmem_call(
        activate_kernel,
        (struct((64, 256), BF16), struct((8, 2 * PLANE), BF16)),
        [pltpu.VMEM((224, 4 * PLANE), F32), pltpu.VMEM((64, 256), F32)],
    )(hidden, second_rows, wide(second_bias), cot)

    low = shifted(dpre[:, PLANE:], 1)
    high = shifted(dpre[:, :PLANE], -1)
    share, raw_second = vmem_call(
        mix_back_kernel,
        (struct((LANE, 2 * PLANE), BF16), struct((256, LANE), F32)),
        [pltpu.VMEM((256, 2 * PLANE), F32), pltpu.VMEM((256, 2 * PLANE), BF16)],
    )(low, dpre, high, hidden[:, PLANE : 3 * PLANE], second_turned)
    parts = lax.all_to_all(share.reshape(16, 8, 2 * PLANE), "filt", 0, 0, tiled=True)

    dhidden, message = vmem_call(
        lift_back_kernel,
        (struct((8, 2 * PLANE), BF16), struct((NEAR, 160, LANE), BF16)),
        [pltpu.VMEM((256, 256), F32), pltpu.VMEM((512, 256), F32), pltpu.VMEM((256, LANE), F32)],
    )(parts, source, raw_second)

    low = shifted(dhidden[:, PLANE:], 1)
    high = shifted(dhidden[:, :PLANE], -1)
    message = near_exchange(message)
    mine = vmem_call(sum_kernel, struct((160, LANE), BF16))(message)
    far = [shifted(mine, NEAR * i) for i in (1, 2, 3)]
    share = vmem_call(
        lift_input_kernel, struct((256, 256), BF16), [pltpu.VMEM((512, 256), F32)]
    )(low, dhidden, high, first_turned)
    share = lax.all_to_all(share.reshape(16, 16, 256), "filt", 0, 0, tiled=True)
    mine = mine.astype(F32)
    for other in far:
        mine = mine + other.astype(F32)
    message = near_exchange(jnp.broadcast_to(mine.astype(BF16)[None], (NEAR, 160, LANE)))
    grad_volume = vmem_call(sum_kernel, struct((16, 256), BF16))(share)

    total_cells = volume.shape[0] * lax.axis_size("space") * 8 * volume.shape[2] * volume.shape[3]
    scale = 1.0 / math.sqrt(total_cells)
    first, second, bias = vmem_call(
        lambda *refs: finish_kernel(scale, *refs),
        (struct((8, 64, 256), F32), struct((216, LANE), F32), struct((16, LANE), F32)),
        [pltpu.VMEM((512, LANE), F32), pltpu.VMEM((512, LANE), F32), pltpu.VMEM((256, LANE), F32)],
    )(message)
    return (
        result.reshape(2, 8, 4, 256),
        grad_volume.reshape(1, 16, 2, 128),
        first,
        bias[8:16, 0],
        second.reshape(27, 8, LANE).transpose(1, 0, 2),
        bias[0:8, 0],
    )


def solution(mesh):
    placed = (
        P("space", "filt", None, None),
        P("filt", None, None),
        P("filt"),
        P("filt", None, None),
        P("filt"),
        P("space", "filt", None, None),
    )
    return jax.shard_map(
        per_device,
        mesh=mesh,
        in_specs=placed,
        out_specs=(
            P("space", "filt", None, None),
            P("space", "filt", None, None),
            P("filt", None, None),
            P("filt"),
            P("filt", None, None),
            P("filt"),
        ),
        check_vma=False,
    )
```

```python
import math

import jax
import jax.numpy as jnp
from jax import lax
from jax.experimental import pallas as pl
from jax.experimental.pallas import tpu as pltpu
from jax.sharding import PartitionSpec as P

F32 = jnp.float32
BF16 = jnp.bfloat16
TAP_PLACE = ((1, 1), (0, 0), (1, 0), (0, -1))
LANE = 128
PLANE = 1024
NEAR = 8


def vmem_call(body, outs, scratch=(), limit=24 * 1024 * 1024):
    return pl.pallas_call(
        body,
        out_shape=outs,
        scratch_shapes=list(scratch),
        compiler_params=pltpu.CompilerParams(vmem_limit_bytes=limit),
    )


def ahead(value, step):
    extent = value.shape[-1]
    return value if step == 0 else pltpu.roll(value, (-step) % extent, value.ndim - 1)


def dot(a, b, dims=((1,), (0,))):
    return lax.dot_general(a, b, (dims, ((), ())), preferred_element_type=F32)


def hidden_kernel(weight, source, bias, out, taps):
    taps[...] = dot(weight[...], source[...])

    def tap(kz, kx, ky, plane, xi):
        row = (kz * 16 + kx * 4 + ky) * 8
        col = plane * 256 + xi * LANE
        return taps[row : row + 8, col : col + LANE]

    for plane in range(4):
        parity_z = (plane + 1) % 2
        base_z = (plane + 1) // 2
        along_z = [(k, base_z + off) for k, (par, off) in enumerate(TAP_PLACE) if par == parity_z]
        for x in range(4):
            along_x = [
                (k, (x // 2 + off) % 2) for k, (par, off) in enumerate(TAP_PLACE) if par == x % 2
            ]
            for parity_y in range(2):
                total = bias[...]
                for ky, (par, off) in enumerate(TAP_PLACE):
                    if par != parity_y:
                        continue
                    part = None
                    for kz, iz in along_z:
                        for kx, ix in along_x:
                            term = tap(kz, kx, ky, iz, ix)
                            part = term if part is None else part + term
                    total = total + ahead(part, off)
                col = plane * PLANE + x * 256 + parity_y * LANE
                value = total.astype(BF16)
                for copy in range(out.shape[0]):
                    out[copy, :, col : col + LANE] = value


def spread_rows(rows, cols):
    natural = lax.broadcasted_iota(jnp.int32, (rows, cols), 0)
    split = lax.broadcasted_iota(jnp.int32, (rows, cols), 1)
    return jnp.where(natural == 2 * (split % LANE) + split // LANE, 1.0, 0.0).astype(BF16)


def split_kernel(field, out, rows):
    rows[...] = dot(field[...], spread_rows(256, 256))
    for z in range(2):
        for x in range(4):
            col = z * PLANE + x * 256
            for e in range(8):
                line = z * 32 + e * 4 + x
                out[e : e + 1, col : col + 256] = rows[line : line + 1, :]


def activate_kernel(hidden, weight, bias, cot, result, dpre, taps, rows):
    taps[...] = dot(weight[...], hidden[...])

    def column(plane, x, parity):
        return plane * PLANE + (x % 4) * 256 + parity * LANE

    for z in range(2):
        for x in range(4):
            halves = []
            for parity in range(2):
                pre = bias[...]
                for ty in (-1, 0, 1):
                    other = (parity + ty) % 2
                    step = (parity + ty) // 2
                    part = None
                    for tz in range(3):
                        for tx in range(3):
                            row = (tz * 9 + tx * 3 + ty + 1) * 8
                            col = column(z + tz, x + tx - 1, other)
                            term = taps[row : row + 8, col : col + LANE]
                            part = term if part is None else part + term
                    pre = pre + ahead(part, step)
                sigma = 1.0 / (1.0 + jnp.exp(-pre))
                halves.append((pre * sigma).astype(BF16))
                col = column(z, x, parity)
                slope = cot[:, col : col + LANE] * sigma * (1.0 + pre * (1.0 - sigma))
                dpre[:, col : col + LANE] = slope.astype(BF16)
            both = jnp.concatenate(halves, axis=1)
            natural = dot(both, spread_rows(256, 256), ((1,), (1,)))
            for e in range(8):
                line = z * 32 + e * 4 + x
                rows[line : line + 1, :] = natural[e : e + 1, :]
    result[...] = rows[...].astype(BF16)


def mix_back_kernel(low, dpre, high, hidden, weight, share, raw, cols, colb):
    planes = (
        low[...].astype(F32),
        dpre[:, :PLANE].astype(F32),
        dpre[:, PLANE:].astype(F32),
        high[...].astype(F32),
    )

    def cells(plane, x, parity):
        col = (x % 4) * 256 + parity * LANE
        return planes[plane][:, col : col + LANE]

    for z in range(2):
        for tz in range(3):
            for x in range(4):
                for parity in range(2):
                    for ty in (-1, 0, 1):
                        other = (parity - ty) % 2
                        step = (parity - ty) // 2
                        for tx in range(3):
                            value = ahead(cells(z + 2 - tz, x - (tx - 1), other), step)
                            row = (tz * 9 + tx * 3 + ty + 1) * 8
                            col = z * PLANE + x * 256 + parity * LANE
                            cols[row : row + 8, col : col + LANE] = value
    cols[216:256, :] = jnp.zeros((40, 2 * PLANE), F32)
    colb[...] = cols[...].astype(BF16)
    share[...] = dot(weight[...], colb[...]).astype(BF16)
    raw[...] = dot(colb[...], hidden[...], ((1,), (1,)))
    total = jnp.sum(planes[1] + planes[2], axis=1, keepdims=True)
    raw[216:224, :] = jnp.broadcast_to(total, (8, LANE))


def pick_columns(field, out, base):
    for kx in range(4):
        for ky in range(4):
            parity, step = (ky - 1) % 2, (ky - 1) // 2
            for xi in range(2):
                x = (2 * xi - 1 + kx) % 4
                col = x * 256 + parity * LANE
                row = base + (kx * 4 + ky) * 8
                out[row : row + 8, xi * LANE : (xi + 1) * LANE] = ahead(
                    field[:, col : col + LANE], step
                )


def lift_back_kernel(parts, source, raw_second, dhidden, message, cols, raw, second):
    total = parts[0].astype(F32)
    for f in range(1, 16):
        total = total + parts[f].astype(F32)
    rounded = total.astype(BF16)
    dhidden[...] = rounded
    total = rounded.astype(F32)
    pick_columns(total[:, :PLANE], cols, 0)
    pick_columns(total[:, PLANE:], cols, LANE)
    for kz, (plane, place) in enumerate(((1, 2), (0, 1), (1, 1), (0, 0))):
        raw[kz * LANE : (kz + 1) * LANE, :] = dot(
            cols[plane * LANE : (plane + 1) * LANE, :].astype(BF16),
            source[:, place * 256 : (place + 1) * 256],
            ((1,), (1,)),
        )
    second[...] = raw_second[...]
    sums = (second[216:224, :], jnp.broadcast_to(jnp.sum(total, axis=1, keepdims=True), (8, LANE)))
    for i, value in enumerate(sums):
        high = value.astype(BF16).astype(F32)
        second[216 + 16 * i : 224 + 16 * i, :] = high
        second[224 + 16 * i : 232 + 16 * i, :] = value - high
    for i in range(NEAR):
        block = raw[64 * i : 64 * (i + 1), :].astype(BF16)
        message[i, 0:64, :] = block[:, :LANE]
        message[i, 64:128, :] = block[:, LANE:]
        message[i, 128:160, :] = second[32 * i : 32 * (i + 1), :].astype(BF16)


def lift_input_kernel(low, dhidden, high, weight, share, cols):
    own = dhidden[...].astype(F32)
    pick_columns(low[...].astype(F32), cols, 0)
    pick_columns(own[:, :PLANE], cols, LANE)
    pick_columns(own[:, PLANE:], cols, 2 * LANE)
    pick_columns(high[...].astype(F32), cols, 3 * LANE)
    share[...] = dot(weight[...], cols[...].astype(BF16)).astype(BF16)


def sum_kernel(parts, out):
    total = parts[0].astype(F32)
    for i in range(1, parts.shape[0]):
        total = total + parts[i].astype(F32)
    out[...] = total.astype(out.dtype)


def pair_kernel(one, other, out):
    total = (one[...].astype(F32) + other[...].astype(F32)).astype(BF16)
    out[...] = jnp.broadcast_to(total, out.shape)


def as_row(column):
    here = lax.broadcasted_iota(jnp.int32, (8, LANE), 0)
    lane = lax.broadcasted_iota(jnp.int32, (8, LANE), 1)
    return jnp.sum(jnp.where(here == lane, column, 0.0), axis=0, keepdims=True)[:, :8]


def finish_kernel(scale, parts, first, second, first_bias, second_bias, left, right, rest):
    for i in range(NEAR):
        left[64 * i : 64 * (i + 1), :] = parts[i, 0:64, :].astype(F32) * scale
        right[64 * i : 64 * (i + 1), :] = parts[i, 64:128, :].astype(F32) * scale
        rest[32 * i : 32 * (i + 1), :] = parts[i, 128:160, :].astype(F32) * scale
    for d in range(8):
        first[d, :, :LANE] = left[pl.ds(d, 64, stride=8), :]
        first[d, :, LANE:] = right[pl.ds(d, 64, stride=8), :]
    second[...] = rest[0:216, :]
    second_bias[...] = as_row(rest[216:224, :] + rest[224:232, :])
    first_bias[...] = as_row(rest[232:240, :] + rest[240:248, :])


def shifted(value, step):
    count = lax.axis_size("space")
    return lax.ppermute(value, "space", [(i, (i + step) % count) for i in range(count)])


def gathered(value):
    copies = jnp.broadcast_to(value[None], (lax.axis_size("filt"),) + value.shape)
    return lax.all_to_all(copies, "filt", 0, 0, tiled=True)


def partner(value, ends):
    count = lax.axis_size("space")
    groups = count // NEAR
    pairs = []
    for i in range(count):
        group = i // NEAR
        other = ((group + ends) ^ 1) - ends
        pairs.append((i, other % groups * NEAR + i % NEAR))
    return lax.ppermute(value, "space", pairs)


def near_exchange(value):
    count = lax.axis_size("space")
    groups = [[g + i for i in range(NEAR)] for g in range(0, count, NEAR)]
    return lax.all_to_all(value, "space", 0, 0, axis_index_groups=groups, tiled=True)


def per_device(volume, first_weight, first_bias, second_weight, second_bias, cotangent):
    struct = jax.ShapeDtypeStruct
    count = lax.axis_size("filt")
    wide = lambda bias: jnp.broadcast_to(bias.astype(F32)[:, None], (8, LANE))
    first_rows = first_weight.transpose(1, 0, 2).reshape(512, 256)
    first_turned = first_weight.transpose(2, 1, 0).reshape(256, 512)
    second_rows = second_weight.transpose(1, 0, 2).reshape(216, LANE)
    second_rows = jnp.pad(second_rows, ((0, 8), (0, 0)))
    second_turned = jnp.pad(second_weight.transpose(2, 1, 0).reshape(LANE, 216), ((0, 0), (0, 40)))

    own = volume.reshape(16, 256)
    source = jnp.concatenate([shifted(own, 1), own, shifted(own, -1)], axis=1)
    source = gathered(source).reshape(256, 768)
    cot = vmem_call(
        split_kernel, struct((8, 2 * PLANE), F32), [pltpu.VMEM((64, 256), F32)]
    )(cotangent.reshape(64, 256))
    hidden = vmem_call(
        hidden_kernel, struct((count, 8, 4 * PLANE), BF16), [pltpu.VMEM((512, 768), F32)]
    )(first_rows, source, wide(first_bias))
    hidden = lax.all_to_all(hidden, "filt", 0, 0, tiled=True).reshape(LANE, 4 * PLANE)

    result, dpre = vmem_call(
        activate_kernel,
        (struct((64, 256), BF16), struct((8, 2 * PLANE), BF16)),
        [pltpu.VMEM((224, 4 * PLANE), F32), pltpu.VMEM((64, 256), F32)],
    )(hidden, second_rows, wide(second_bias), cot)

    low = shifted(dpre[:, PLANE:], 1)
    high = shifted(dpre[:, :PLANE], -1)
    share, raw_second = vmem_call(
        mix_back_kernel,
        (struct((LANE, 2 * PLANE), BF16), struct((256, LANE), F32)),
        [pltpu.VMEM((256, 2 * PLANE), F32), pltpu.VMEM((256, 2 * PLANE), BF16)],
    )(low, dpre, high, hidden[:, PLANE : 3 * PLANE], second_turned)
    parts = lax.all_to_all(share.reshape(16, 8, 2 * PLANE), "filt", 0, 0, tiled=True)

    dhidden, message = vmem_call(
        lift_back_kernel,
        (struct((8, 2 * PLANE), BF16), struct((NEAR, 160, LANE), BF16)),
        [pltpu.VMEM((256, 256), F32), pltpu.VMEM((512, 256), F32), pltpu.VMEM((256, LANE), F32)],
    )(parts, source, raw_second)

    low = shifted(dhidden[:, PLANE:], 1)
    high = shifted(dhidden[:, :PLANE], -1)
    message = near_exchange(message)
    message, low, high = lax.optimization_barrier((message, low, high))
    mine = vmem_call(sum_kernel, struct((160, LANE), BF16))(message)
    other = partner(mine, 0)
    share = vmem_call(
        lift_input_kernel, struct((256, 256), BF16), [pltpu.VMEM((512, 256), F32)]
    )(low, dhidden, high, first_turned)
    mine = vmem_call(pair_kernel, struct((160, LANE), BF16))(mine, other)
    mine, share = lax.optimization_barrier((mine, share))
    other = partner(mine, 1)
    share = lax.all_to_all(share.reshape(16, 16, 256), "filt", 0, 0, tiled=True)
    other, share = lax.optimization_barrier((other, share))
    message = vmem_call(pair_kernel, struct((NEAR, 160, LANE), BF16))(mine, other)
    message = near_exchange(message)
    grad_volume = vmem_call(sum_kernel, struct((16, 256), BF16))(share)

    total_cells = volume.shape[0] * lax.axis_size("space") * 8 * volume.shape[2] * volume.shape[3]
    scale = 1.0 / math.sqrt(total_cells)
    first, second, sum_first, sum_second = vmem_call(
        lambda *refs: finish_kernel(scale, *refs),
        (
            struct((8, 64, 256), F32),
            struct((216, LANE), F32),
            struct((1, 8), F32),
            struct((1, 8), F32),
        ),
        [pltpu.VMEM((512, LANE), F32), pltpu.VMEM((512, LANE), F32), pltpu.VMEM((256, LANE), F32)],
    )(message)
    return (
        result.reshape(2, 8, 4, 256),
        grad_volume.reshape(1, 16, 2, 128),
        first,
        sum_first.reshape(8),
        second.reshape(27, 8, LANE).transpose(1, 0, 2),
        sum_second.reshape(8),
    )


def solution(mesh):
    placed = (
        P("space", "filt", None, None),
        P("filt", None, None),
        P("filt"),
        P("filt", None, None),
        P("filt"),
        P("space", "filt", None, None),
    )
    return jax.shard_map(
        per_device,
        mesh=mesh,
        in_specs=placed,
        out_specs=(
            P("space", "filt", None, None),
            P("space", "filt", None, None),
            P("filt", None, None),
            P("filt"),
            P("filt", None, None),
            P("filt"),
        ),
        check_vma=False,
    )
```

```python
import math

import jax
import jax.numpy as jnp
from jax import lax
from jax.experimental import pallas as pl
from jax.experimental.pallas import tpu as pltpu
from jax.sharding import PartitionSpec as P

F32 = jnp.float32
BF16 = jnp.bfloat16
TAP_PLACE = ((1, 1), (0, 0), (1, 0), (0, -1))
LANE = 128
PLANE = 1024
NEAR = 8


def vmem_call(body, outs, scratch=(), limit=24 * 1024 * 1024):
    return pl.pallas_call(
        body,
        out_shape=outs,
        scratch_shapes=list(scratch),
        compiler_params=pltpu.CompilerParams(vmem_limit_bytes=limit),
    )


def ahead(value, step):
    extent = value.shape[-1]
    return value if step == 0 else pltpu.roll(value, (-step) % extent, value.ndim - 1)


def dot(a, b, dims=((1,), (0,))):
    return lax.dot_general(a, b, (dims, ((), ())), preferred_element_type=F32)


def hidden_kernel(weight, source, bias, out, taps):
    taps[...] = dot(weight[...], source[...])

    def tap(kz, kx, ky, plane, xi):
        row = (kz * 16 + kx * 4 + ky) * 8
        col = plane * 256 + xi * LANE
        return taps[row : row + 8, col : col + LANE]

    for plane in range(4):
        parity_z = (plane + 1) % 2
        base_z = (plane + 1) // 2
        along_z = [(k, base_z + off) for k, (par, off) in enumerate(TAP_PLACE) if par == parity_z]
        for x in range(4):
            along_x = [
                (k, (x // 2 + off) % 2) for k, (par, off) in enumerate(TAP_PLACE) if par == x % 2
            ]
            for parity_y in range(2):
                total = bias[...]
                for ky, (par, off) in enumerate(TAP_PLACE):
                    if par != parity_y:
                        continue
                    part = None
                    for kz, iz in along_z:
                        for kx, ix in along_x:
                            term = tap(kz, kx, ky, iz, ix)
                            part = term if part is None else part + term
                    total = total + ahead(part, off)
                col = plane * PLANE + x * 256 + parity_y * LANE
                value = total.astype(BF16)
                for copy in range(out.shape[0]):
                    out[copy, :, col : col + LANE] = value


def spread_rows(rows, cols):
    natural = lax.broadcasted_iota(jnp.int32, (rows, cols), 0)
    split = lax.broadcasted_iota(jnp.int32, (rows, cols), 1)
    return jnp.where(natural == 2 * (split % LANE) + split // LANE, 1.0, 0.0).astype(BF16)


def split_kernel(field, out, rows):
    rows[...] = dot(field[...], spread_rows(256, 256))
    for z in range(2):
        for x in range(4):
            col = z * PLANE + x * 256
            for e in range(8):
                line = z * 32 + e * 4 + x
                out[e : e + 1, col : col + 256] = rows[line : line + 1, :]


def activate_kernel(
    hidden, weight, bias, cot, turned, result, share, raw, taps, rows, dpre, cols
):
    taps[...] = dot(weight[...], hidden[...])

    def column(plane, x, parity):
        return plane * PLANE + (x % 4) * 256 + parity * LANE

    for z in range(2):
        for x in range(4):
            halves = []
            for parity in range(2):
                pre = bias[...]
                for ty in (-1, 0, 1):
                    other = (parity + ty) % 2
                    step = (parity + ty) // 2
                    part = None
                    for tz in range(3):
                        for tx in range(3):
                            row = (tz * 9 + tx * 3 + ty + 1) * 8
                            col = column(z + tz, x + tx - 1, other)
                            term = taps[row : row + 8, col : col + LANE]
                            part = term if part is None else part + term
                    pre = pre + ahead(part, step)
                sigma = 1.0 / (1.0 + jnp.exp(-pre))
                halves.append((pre * sigma).astype(BF16))
                col = column(z, x, parity)
                slope = cot[:, col : col + LANE] * sigma * (1.0 + pre * (1.0 - sigma))
                dpre[:, col : col + LANE] = slope.astype(BF16).astype(F32)
            both = jnp.concatenate(halves, axis=1)
            natural = dot(both, spread_rows(256, 256), ((1,), (1,)))
            for e in range(8):
                line = z * 32 + e * 4 + x
                rows[line : line + 1, :] = natural[e : e + 1, :]
    result[...] = rows[...].astype(BF16)

    for z in range(2):
        cols[z * LANE + 72 : (z + 1) * LANE, :] = jnp.zeros((LANE - 72, PLANE), F32)
        for x in range(4):
            for parity in range(2):
                for ty in (-1, 0, 1):
                    other = (parity - ty) % 2
                    step = (parity - ty) // 2
                    for tx in range(3):
                        col = column(z, x - (tx - 1), other)
                        value = ahead(dpre[:, col : col + LANE], step)
                        row = z * LANE + (tx * 3 + ty + 1) * 8
                        col = column(0, x, parity)
                        cols[row : row + 8, col : col + LANE] = value
    moved = cols[...].astype(BF16)
    lower, upper = moved[:LANE], moved[LANE:]
    share[:, :PLANE] = dot(turned[:, 2 * LANE :], lower).astype(BF16)
    share[:, PLANE : 2 * PLANE] = dot(turned[:, LANE:], moved).astype(BF16)
    share[:, 2 * PLANE : 3 * PLANE] = dot(turned[:, : 2 * LANE], moved).astype(BF16)
    share[:, 3 * PLANE :] = dot(turned[:, :LANE], upper).astype(BF16)
    for tz in range(3):
        one = dot(lower, hidden[:, tz * PLANE : (tz + 1) * PLANE], ((1,), (1,)))
        two = dot(upper, hidden[:, (tz + 1) * PLANE : (tz + 2) * PLANE], ((1,), (1,)))
        raw[tz * 72 : (tz + 1) * 72, :] = (one + two)[:72]
    total = jnp.sum(dpre[...], axis=1, keepdims=True)
    raw[216:224, :] = jnp.broadcast_to(total, (8, LANE))
    raw[224:256, :] = jnp.zeros((32, LANE), F32)


def pick_columns(field, out, base):
    for kx in range(4):
        for ky in range(4):
            parity, step = (ky - 1) % 2, (ky - 1) // 2
            for xi in range(2):
                x = (2 * xi - 1 + kx) % 4
                col = x * 256 + parity * LANE
                row = base + (kx * 4 + ky) * 8
                out[row : row + 8, xi * LANE : (xi + 1) * LANE] = ahead(
                    field[:, col : col + LANE], step
                )


def lift_back_kernel(parts, source, raw_second, low, high, message, cols, raw, second):
    total = parts[0].astype(F32)
    for f in range(1, parts.shape[0]):
        total = total + parts[f].astype(F32)
    low[...] = total[:, : 2 * PLANE]
    high[...] = total[:, 2 * PLANE :]
    for plane in range(4):
        pick_columns(total[:, plane * PLANE : (plane + 1) * PLANE], cols, plane * LANE)
    pairs = (((0, 1), (2, 2)), ((1, 1), (3, 2)), ((0, 0), (2, 1)), ((1, 0), (3, 1)))
    for kz, met in enumerate(pairs):
        part = None
        for plane, place in met:
            term = dot(
                cols[plane * LANE : (plane + 1) * LANE, :].astype(BF16),
                source[:, place * 256 : (place + 1) * 256],
                ((1,), (1,)),
            )
            part = term if part is None else part + term
        raw[kz * LANE : (kz + 1) * LANE, :] = part
    second[...] = raw_second[...]
    sums = (second[216:224, :], jnp.broadcast_to(jnp.sum(total, axis=1, keepdims=True), (8, LANE)))
    for i, value in enumerate(sums):
        high = value.astype(BF16).astype(F32)
        second[216 + 16 * i : 224 + 16 * i, :] = high
        second[224 + 16 * i : 232 + 16 * i, :] = value - high
    for i in range(NEAR):
        block = raw[64 * i : 64 * (i + 1), :].astype(BF16)
        message[i, 0:64, :] = block[:, :LANE]
        message[i, 64:128, :] = block[:, LANE:]
        message[i, 128:160, :] = second[32 * i : 32 * (i + 1), :].astype(BF16)


def lift_input_kernel(low, low_other, high, high_other, weight, share, cols):
    for half, (one, other) in enumerate(((low, low_other), (high, high_other))):
        total = (one[...] + other[...]).astype(BF16).astype(F32)
        pick_columns(total[:, :PLANE], cols, 2 * half * LANE)
        pick_columns(total[:, PLANE:], cols, (2 * half + 1) * LANE)
    share[...] = dot(weight[...], cols[...].astype(BF16)).astype(BF16)


def sum_kernel(parts, out):
    total = parts[0].astype(F32)
    for i in range(1, parts.shape[0]):
        total = total + parts[i].astype(F32)
    out[...] = total.astype(out.dtype)


def pair_kernel(one, other, out):
    total = (one[...].astype(F32) + other[...].astype(F32)).astype(BF16)
    out[...] = jnp.broadcast_to(total, out.shape)


def as_row(column):
    here = lax.broadcasted_iota(jnp.int32, (8, LANE), 0)
    lane = lax.broadcasted_iota(jnp.int32, (8, LANE), 1)
    return jnp.sum(jnp.where(here == lane, column, 0.0), axis=0, keepdims=True)[:, :8]


def finish_kernel(scale, parts, first, second, first_bias, second_bias, left, right, rest):
    for i in range(NEAR):
        left[64 * i : 64 * (i + 1), :] = parts[i, 0:64, :].astype(F32) * scale
        right[64 * i : 64 * (i + 1), :] = parts[i, 64:128, :].astype(F32) * scale
        rest[32 * i : 32 * (i + 1), :] = parts[i, 128:160, :].astype(F32) * scale
    for d in range(8):
        first[d, :, :LANE] = left[pl.ds(d, 64, stride=8), :]
        first[d, :, LANE:] = right[pl.ds(d, 64, stride=8), :]
    second[...] = rest[0:216, :]
    second_bias[...] = as_row(rest[216:224, :] + rest[224:232, :])
    first_bias[...] = as_row(rest[232:240, :] + rest[240:248, :])


def shifted(value, step):
    count = lax.axis_size("space")
    return lax.ppermute(value, "space", [(i, (i + step) % count) for i in range(count)])


def gathered(value):
    copies = jnp.broadcast_to(value[None], (lax.axis_size("filt"),) + value.shape)
    return lax.all_to_all(copies, "filt", 0, 0, tiled=True)


def partner(value, ends):
    count = lax.axis_size("space")
    groups = count // NEAR
    pairs = []
    for i in range(count):
        group = i // NEAR
        other = ((group + ends) ^ 1) - ends
        pairs.append((i, other % groups * NEAR + i % NEAR))
    return lax.ppermute(value, "space", pairs)


def near_exchange(value):
    count = lax.axis_size("space")
    groups = [[g + i for i in range(NEAR)] for g in range(0, count, NEAR)]
    return lax.all_to_all(value, "space", 0, 0, axis_index_groups=groups, tiled=True)


def per_device(volume, first_weight, first_bias, second_weight, second_bias, cotangent):
    struct = jax.ShapeDtypeStruct
    count = lax.axis_size("filt")
    wide = lambda bias: jnp.broadcast_to(bias.astype(F32)[:, None], (8, LANE))
    first_rows = first_weight.transpose(1, 0, 2).reshape(512, 256)
    first_turned = first_weight.transpose(2, 1, 0).reshape(256, 512)
    second_rows = second_weight.transpose(1, 0, 2).reshape(216, LANE)
    second_rows = jnp.pad(second_rows, ((0, 8), (0, 0)))
    second_turned = second_weight.transpose(2, 1, 0).reshape(LANE, 3, 72)[:, ::-1]
    second_turned = jnp.pad(second_turned, ((0, 0), (0, 0), (0, 56))).reshape(LANE, 384)

    source = jnp.concatenate([shifted(volume, 1), volume, shifted(volume, -1)], axis=0)
    source = source.transpose(1, 0, 2, 3).reshape(16, 768)
    source = gathered(source).reshape(256, 768)
    cot = vmem_call(
        split_kernel, struct((8, 2 * PLANE), F32), [pltpu.VMEM((64, 256), F32)]
    )(cotangent.reshape(64, 256))
    hidden = vmem_call(
        hidden_kernel, struct((count, 8, 4 * PLANE), BF16), [pltpu.VMEM((512, 768), F32)]
    )(first_rows, source, wide(first_bias))
    hidden = lax.all_to_all(hidden, "filt", 0, 0, tiled=True).reshape(LANE, 4 * PLANE)

    result, share, raw_second = vmem_call(
        activate_kernel,
        (
            struct((64, 256), BF16),
            struct((LANE, 4 * PLANE), BF16),
            struct((256, LANE), F32),
        ),
        [
            pltpu.VMEM((224, 4 * PLANE), F32),
            pltpu.VMEM((64, 256), F32),
            pltpu.VMEM((8, 2 * PLANE), F32),
            pltpu.VMEM((256, PLANE), F32),
        ],
    )(hidden, second_rows, wide(second_bias), cot, second_turned)
    parts = lax.all_to_all(share.reshape(16, 8, 4 * PLANE), "filt", 0, 0, tiled=True)

    low, high, message = vmem_call(
        lift_back_kernel,
        (
            struct((8, 2 * PLANE), F32),
            struct((8, 2 * PLANE), F32),
            struct((NEAR, 160, LANE), BF16),
        ),
        [pltpu.VMEM((512, 256), F32), pltpu.VMEM((512, 256), F32), pltpu.VMEM((256, LANE), F32)],
    )(parts, source, raw_second)

    low_other = shifted(high, 1)
    high_other = shifted(low, -1)
    message = near_exchange(message)
    message, low_other, high_other = lax.optimization_barrier((message, low_other, high_other))
    mine = vmem_call(sum_kernel, struct((160, LANE), BF16))(message)
    other = partner(mine, 0)
    share = vmem_call(
        lift_input_kernel, struct((256, 256), BF16), [pltpu.VMEM((512, 256), F32)]
    )(low, low_other, high, high_other, first_turned)
    mine = vmem_call(pair_kernel, struct((160, LANE), BF16))(mine, other)
    mine, share = lax.optimization_barrier((mine, share))
    other = partner(mine, 1)
    share = lax.all_to_all(share.reshape(16, 16, 256), "filt", 0, 0, tiled=True)
    other, share = lax.optimization_barrier((other, share))
    message = vmem_call(pair_kernel, struct((NEAR, 160, LANE), BF16))(mine, other)
    message = near_exchange(message)
    grad_volume = vmem_call(sum_kernel, struct((16, 256), BF16))(share)

    total_cells = volume.shape[0] * lax.axis_size("space") * 8 * volume.shape[2] * volume.shape[3]
    scale = 1.0 / math.sqrt(total_cells)
    first, second, sum_first, sum_second = vmem_call(
        lambda *refs: finish_kernel(scale, *refs),
        (
            struct((8, 64, 256), F32),
            struct((216, LANE), F32),
            struct((1, 8), F32),
            struct((1, 8), F32),
        ),
        [pltpu.VMEM((512, LANE), F32), pltpu.VMEM((512, LANE), F32), pltpu.VMEM((256, LANE), F32)],
    )(message)
    return (
        result.reshape(2, 8, 4, 256),
        grad_volume.reshape(1, 16, 2, 128),
        first,
        sum_first.reshape(8),
        second.reshape(27, 8, LANE).transpose(1, 0, 2),
        sum_second.reshape(8),
    )


def solution(mesh):
    placed = (
        P("space", "filt", None, None),
        P("filt", None, None),
        P("filt"),
        P("filt", None, None),
        P("filt"),
        P("space", "filt", None, None),
    )
    return jax.shard_map(
        per_device,
        mesh=mesh,
        in_specs=placed,
        out_specs=(
            P("space", "filt", None, None),
            P("space", "filt", None, None),
            P("filt", None, None),
            P("filt"),
            P("filt", None, None),
            P("filt"),
        ),
        check_vma=False,
    )
```

```python
import math

import jax
import jax.numpy as jnp
from jax import lax
from jax.experimental import pallas as pl
from jax.experimental.pallas import tpu as pltpu
from jax.sharding import PartitionSpec as P

F32 = jnp.float32
BF16 = jnp.bfloat16
TAP_PLACE = ((1, 1), (0, 0), (1, 0), (0, -1))
LANE = 128
PLANE = 1024
NEAR = 8


def vmem_call(body, outs, scratch=(), specs=None, limit=24 * 1024 * 1024):
    return pl.pallas_call(
        body,
        out_shape=outs,
        **({} if specs is None else {"in_specs": specs}),
        scratch_shapes=list(scratch),
        compiler_params=pltpu.CompilerParams(vmem_limit_bytes=limit),
    )


def ahead(value, step):
    extent = value.shape[-1]
    return value if step == 0 else pltpu.roll(value, (-step) % extent, value.ndim - 1)


def dot(a, b, dims=((1,), (0,))):
    return lax.dot_general(a, b, (dims, ((), ())), preferred_element_type=F32)


def hidden_kernel(odd, weight, pair, outer, bias, source, out, taps):
    @pl.when(odd[0] == 0)
    def _():
        source[:, :256] = outer[...]
        source[:, 256:512] = pair[:256]
        source[:, 512:] = pair[256:]

    @pl.when(odd[0] == 1)
    def _():
        source[:, :256] = pair[:256]
        source[:, 256:512] = pair[256:]
        source[:, 512:] = outer[...]

    taps[...] = dot(weight[...], source[...])

    def tap(kz, kx, ky, plane, xi):
        row = (kz * 16 + kx * 4 + ky) * 8
        col = plane * 256 + xi * LANE
        return taps[row : row + 8, col : col + LANE]

    for plane in range(4):
        parity_z = (plane + 1) % 2
        base_z = (plane + 1) // 2
        along_z = [(k, base_z + off) for k, (par, off) in enumerate(TAP_PLACE) if par == parity_z]
        for x in range(4):
            along_x = [
                (k, (x // 2 + off) % 2) for k, (par, off) in enumerate(TAP_PLACE) if par == x % 2
            ]
            for parity_y in range(2):
                total = bias[...]
                for ky, (par, off) in enumerate(TAP_PLACE):
                    if par != parity_y:
                        continue
                    part = None
                    for kz, iz in along_z:
                        for kx, ix in along_x:
                            term = tap(kz, kx, ky, iz, ix)
                            part = term if part is None else part + term
                    total = total + ahead(part, off)
                col = plane * PLANE + x * 256 + parity_y * LANE
                value = total.astype(BF16)
                for copy in range(out.shape[0]):
                    out[copy, :, col : col + LANE] = value


def spread_rows(rows, cols):
    natural = lax.broadcasted_iota(jnp.int32, (rows, cols), 0)
    split = lax.broadcasted_iota(jnp.int32, (rows, cols), 1)
    return jnp.where(natural == 2 * (split % LANE) + split // LANE, 1.0, 0.0).astype(BF16)


def split_kernel(field, out, rows):
    rows[...] = dot(field[...], spread_rows(256, 256))
    for z in range(2):
        for x in range(4):
            col = z * PLANE + x * 256
            for e in range(8):
                line = z * 32 + e * 4 + x
                out[e : e + 1, col : col + 256] = rows[line : line + 1, :]


def activate_kernel(
    near, across, weight, bias, cot, turned, result, own, share, raw, taps, rows, dpre, cols
):
    hidden = jnp.concatenate([near[...], across[...]], axis=0)
    taps[...] = dot(weight[...], hidden)

    def column(plane, x, parity):
        return plane * PLANE + (x % 4) * 256 + parity * LANE

    for z in range(2):
        for x in range(4):
            halves = []
            for parity in range(2):
                pre = bias[...]
                for ty in (-1, 0, 1):
                    other = (parity + ty) % 2
                    step = (parity + ty) // 2
                    part = None
                    for tz in range(3):
                        for tx in range(3):
                            row = (tz * 9 + tx * 3 + ty + 1) * 8
                            col = column(z + tz, x + tx - 1, other)
                            term = taps[row : row + 8, col : col + LANE]
                            part = term if part is None else part + term
                    pre = pre + ahead(part, step)
                sigma = 1.0 / (1.0 + jnp.exp(-pre))
                halves.append((pre * sigma).astype(BF16))
                col = column(z, x, parity)
                slope = cot[:, col : col + LANE] * sigma * (1.0 + pre * (1.0 - sigma))
                dpre[:, col : col + LANE] = slope.astype(BF16).astype(F32)
            both = jnp.concatenate(halves, axis=1)
            natural = dot(both, spread_rows(256, 256), ((1,), (1,)))
            for e in range(8):
                line = z * 32 + e * 4 + x
                rows[line : line + 1, :] = natural[e : e + 1, :]
    result[...] = rows[...].astype(BF16)

    for z in range(2):
        cols[z * LANE + 72 : (z + 1) * LANE, :] = jnp.zeros((LANE - 72, PLANE), F32)
        for x in range(4):
            for parity in range(2):
                for ty in (-1, 0, 1):
                    other = (parity - ty) % 2
                    step = (parity - ty) // 2
                    for tx in range(3):
                        col = column(z, x - (tx - 1), other)
                        value = ahead(dpre[:, col : col + LANE], step)
                        row = z * LANE + (tx * 3 + ty + 1) * 8
                        col = column(0, x, parity)
                        cols[row : row + 8, col : col + LANE] = value
    moved = cols[...].astype(BF16)
    lower, upper = moved[:LANE], moved[LANE:]
    for rows_of, out in ((slice(0, 64), own), (slice(64, 128), share)):
        out[:, :PLANE] = dot(turned[rows_of, 2 * LANE :], lower).astype(BF16)
        out[:, PLANE : 2 * PLANE] = dot(turned[rows_of, LANE:], moved).astype(BF16)
        out[:, 2 * PLANE : 3 * PLANE] = dot(turned[rows_of, : 2 * LANE], moved).astype(BF16)
        out[:, 3 * PLANE :] = dot(turned[rows_of, :LANE], upper).astype(BF16)
    for tz in range(3):
        one = dot(lower, hidden[:, tz * PLANE : (tz + 1) * PLANE], ((1,), (1,)))
        two = dot(upper, hidden[:, (tz + 1) * PLANE : (tz + 2) * PLANE], ((1,), (1,)))
        raw[tz * 72 : (tz + 1) * 72, :] = (one + two)[:72]
    total = jnp.sum(dpre[...], axis=1, keepdims=True)
    raw[216:224, :] = jnp.broadcast_to(total, (8, LANE))
    raw[224:256, :] = jnp.zeros((32, LANE), F32)


def pick_columns(field, out, base):
    for kx in range(4):
        for ky in range(4):
            parity, step = (ky - 1) % 2, (ky - 1) // 2
            for xi in range(2):
                x = (2 * xi - 1 + kx) % 4
                col = x * 256 + parity * LANE
                row = base + (kx * 4 + ky) * 8
                out[row : row + 8, xi * LANE : (xi + 1) * LANE] = ahead(
                    field[:, col : col + LANE], step
                )


def lift_back_kernel(parts, source, raw_second, low, high, message, cols, raw, second):
    total = parts[0].astype(F32)
    for f in range(1, parts.shape[0]):
        total = total + parts[f].astype(F32)
    low[...] = total[:, : 2 * PLANE]
    high[...] = total[:, 2 * PLANE :]
    for plane in range(4):
        pick_columns(total[:, plane * PLANE : (plane + 1) * PLANE], cols, plane * LANE)
    pairs = (((0, 1), (2, 2)), ((1, 1), (3, 2)), ((0, 0), (2, 1)), ((1, 0), (3, 1)))
    for kz, met in enumerate(pairs):
        part = None
        for plane, place in met:
            term = dot(
                cols[plane * LANE : (plane + 1) * LANE, :].astype(BF16),
                source[:, place * 256 : (place + 1) * 256],
                ((1,), (1,)),
            )
            part = term if part is None else part + term
        raw[kz * LANE : (kz + 1) * LANE, :] = part
    second[...] = raw_second[...]
    sums = (second[216:224, :], jnp.broadcast_to(jnp.sum(total, axis=1, keepdims=True), (8, LANE)))
    for i, value in enumerate(sums):
        high = value.astype(BF16).astype(F32)
        second[216 + 16 * i : 224 + 16 * i, :] = high
        second[224 + 16 * i : 232 + 16 * i, :] = value - high
    for i in range(NEAR):
        block = raw[64 * i : 64 * (i + 1), :].astype(BF16)
        message[i, 0:64, :] = block[:, :LANE]
        message[i, 64:128, :] = block[:, LANE:]
        message[i, 128:160, :] = second[32 * i : 32 * (i + 1), :].astype(BF16)


def lift_input_kernel(low, low_other, high, high_other, weight, share, cols):
    for half, (one, other) in enumerate(((low, low_other), (high, high_other))):
        total = (one[...] + other[...]).astype(BF16).astype(F32)
        pick_columns(total[:, :PLANE], cols, 2 * half * LANE)
        pick_columns(total[:, PLANE:], cols, (2 * half + 1) * LANE)
    share[...] = dot(weight[...], cols[...].astype(BF16)).astype(BF16)


def sum_kernel(parts, out):
    total = parts[0].astype(F32)
    for i in range(1, parts.shape[0]):
        total = total + parts[i].astype(F32)
    out[...] = total.astype(out.dtype)


def pair_kernel(one, other, out):
    total = (one[...].astype(F32) + other[...].astype(F32)).astype(BF16)
    out[...] = jnp.broadcast_to(total, out.shape)


def as_row(column):
    here = lax.broadcasted_iota(jnp.int32, (8, LANE), 0)
    lane = lax.broadcasted_iota(jnp.int32, (8, LANE), 1)
    return jnp.sum(jnp.where(here == lane, column, 0.0), axis=0, keepdims=True)[:, :8]


def finish_kernel(scale, parts, order, first, second, first_bias, second_bias, left, right, rest):
    for i in range(NEAR):
        left[64 * i : 64 * (i + 1), :] = parts[i, 0:64, :].astype(F32) * scale
        right[64 * i : 64 * (i + 1), :] = parts[i, 64:128, :].astype(F32) * scale
        rest[32 * i : 32 * (i + 1), :] = parts[i, 128:160, :].astype(F32)
    for d in range(8):
        first[d, :, :LANE] = left[pl.ds(d, 64, stride=8), :]
        first[d, :, LANE:] = right[pl.ds(d, 64, stride=8), :]
    second[...] = dot(rest[...].astype(BF16), order[...])[0:216] * scale
    second_bias[...] = as_row(rest[216:224, :] + rest[224:232, :]) * scale
    first_bias[...] = as_row(rest[232:240, :] + rest[240:248, :]) * scale


def shifted(value, step):
    count = lax.axis_size("space")
    return lax.ppermute(value, "space", [(i, (i + step) % count) for i in range(count)])


def chip_exchange(value):
    count = lax.axis_size("filt")
    groups = [list(range(core, count, 2)) for core in range(2)]
    return lax.all_to_all(value, "filt", 0, 0, axis_index_groups=groups, tiled=True)


def other_core(value):
    count = lax.axis_size("filt")
    return lax.ppermute(value, "filt", [(i, i ^ 1) for i in range(count)])


def pair_gather(value):
    slabs, blocks = lax.axis_size("space"), lax.axis_size("filt")
    groups = [
        [s * blocks + f for s in (low, low + 1) for f in range(blocks)] for low in range(0, slabs, 2)
    ]
    copies = jnp.broadcast_to(value[None], (2 * blocks,) + value.shape)
    return lax.all_to_all(copies, ("space", "filt"), 0, 0, axis_index_groups=groups, tiled=True)


def outer_plane(value):
    count = lax.axis_size("space")
    pairs = [(i, (((i + 1) ^ 1) - 1) % count) for i in range(count)]
    return lax.ppermute(value, "space", pairs)


def by_core(weight, core):
    split = weight.reshape(weight.shape[:-1] + (8, 2, 8))
    split = jnp.where(core == 0, split, jnp.flip(split, -2))
    return jnp.swapaxes(split, -3, -2).reshape(weight.shape)


def partner(value, ends):
    count = lax.axis_size("space")
    groups = count // NEAR
    pairs = []
    for i in range(count):
        group = i // NEAR
        other = ((group + ends) ^ 1) - ends
        pairs.append((i, other % groups * NEAR + i % NEAR))
    return lax.ppermute(value, "space", pairs)


def near_exchange(value):
    count = lax.axis_size("space")
    groups = [[g + i for i in range(NEAR)] for g in range(0, count, NEAR)]
    return lax.all_to_all(value, "space", 0, 0, axis_index_groups=groups, tiled=True)


def per_device(volume, first_weight, first_bias, second_weight, second_bias, cotangent):
    struct = jax.ShapeDtypeStruct
    wide = lambda bias: jnp.broadcast_to(bias.astype(F32)[:, None], (8, LANE))
    core = lax.axis_index("filt") % 2
    odd = lax.axis_index("space") % 2
    first_rows = first_weight.transpose(1, 0, 2).reshape(512, 256)
    first_turned = first_weight.transpose(2, 1, 0).reshape(256, 512)
    second = by_core(second_weight, core)
    second_rows = second.transpose(1, 0, 2).reshape(216, LANE)
    second_rows = jnp.pad(second_rows, ((0, 8), (0, 0)))
    second_turned = second.transpose(2, 1, 0).reshape(LANE, 3, 72)[:, ::-1]
    second_turned = jnp.pad(second_turned, ((0, 0), (0, 0), (0, 56))).reshape(LANE, 384)
    order = by_core(jnp.eye(LANE, dtype=BF16), core).T

    pair = pair_gather(volume.reshape(16, 256)).reshape(2, 256, 256)
    outer = outer_plane(lax.dynamic_index_in_dim(pair, odd, 0, keepdims=False))
    cot = vmem_call(
        split_kernel, struct((8, 2 * PLANE), F32), [pltpu.VMEM((64, 256), F32)]
    )(cotangent.reshape(64, 256))
    whole = pl.BlockSpec(memory_space=pltpu.VMEM)
    source, hidden = vmem_call(
        hidden_kernel,
        (struct((256, 768), BF16), struct((8, 8, 4 * PLANE), BF16)),
        [pltpu.VMEM((512, 768), F32)],
        [pl.BlockSpec(memory_space=pltpu.SMEM)] + [whole] * 4,
    )(odd.reshape(1), first_rows, pair.reshape(512, 256), outer, wide(first_bias))
    hidden = chip_exchange(hidden).reshape(64, 4 * PLANE)

    result, own, share, raw_second = vmem_call(
        activate_kernel,
        (
            struct((64, 256), BF16),
            struct((64, 4 * PLANE), BF16),
            struct((64, 4 * PLANE), BF16),
            struct((256, LANE), F32),
        ),
        [
            pltpu.VMEM((224, 4 * PLANE), F32),
            pltpu.VMEM((64, 256), F32),
            pltpu.VMEM((8, 2 * PLANE), F32),
            pltpu.VMEM((256, PLANE), F32),
        ],
    )(hidden, other_core(hidden), second_rows, wide(second_bias), cot, second_turned)
    share = vmem_call(pair_kernel, struct((64, 4 * PLANE), BF16))(own, other_core(share))
    parts = chip_exchange(share.reshape(8, 8, 4 * PLANE))

    low, high, message = vmem_call(
        lift_back_kernel,
        (
            struct((8, 2 * PLANE), F32),
            struct((8, 2 * PLANE), F32),
            struct((NEAR, 160, LANE), BF16),
        ),
        [pltpu.VMEM((512, 256), F32), pltpu.VMEM((512, 256), F32), pltpu.VMEM((256, LANE), F32)],
    )(parts, source, raw_second)

    low_other = shifted(high, 1)
    high_other = shifted(low, -1)
    message = near_exchange(message)
    message, low_other, high_other = lax.optimization_barrier((message, low_other, high_other))
    mine = vmem_call(sum_kernel, struct((160, LANE), BF16))(message)
    other = partner(mine, 0)
    share = vmem_call(
        lift_input_kernel, struct((256, 256), BF16), [pltpu.VMEM((512, 256), F32)]
    )(low, low_other, high, high_other, first_turned)
    mine = vmem_call(pair_kernel, struct((160, LANE), BF16))(mine, other)
    mine, share = lax.optimization_barrier((mine, share))
    other = partner(mine, 1)
    share = lax.all_to_all(share.reshape(16, 16, 256), "filt", 0, 0, tiled=True)
    other, share = lax.optimization_barrier((other, share))
    message = vmem_call(pair_kernel, struct((NEAR, 160, LANE), BF16))(mine, other)
    message = near_exchange(message)
    grad_volume = vmem_call(sum_kernel, struct((16, 256), BF16))(share)

    total_cells = volume.shape[0] * lax.axis_size("space") * 8 * volume.shape[2] * volume.shape[3]
    scale = 1.0 / math.sqrt(total_cells)
    first, second, sum_first, sum_second = vmem_call(
        lambda *refs: finish_kernel(scale, *refs),
        (
            struct((8, 64, 256), F32),
            struct((216, LANE), F32),
            struct((1, 8), F32),
            struct((1, 8), F32),
        ),
        [pltpu.VMEM((512, LANE), F32), pltpu.VMEM((512, LANE), F32), pltpu.VMEM((256, LANE), F32)],
    )(message, order)
    return (
        result.reshape(2, 8, 4, 256),
        grad_volume.reshape(1, 16, 2, 128),
        first,
        sum_first.reshape(8),
        second.reshape(27, 8, LANE).transpose(1, 0, 2),
        sum_second.reshape(8),
    )


def solution(mesh):
    placed = (
        P("space", "filt", None, None),
        P("filt", None, None),
        P("filt"),
        P("filt", None, None),
        P("filt"),
        P("space", "filt", None, None),
    )
    return jax.shard_map(
        per_device,
        mesh=mesh,
        in_specs=placed,
        out_specs=(
            P("space", "filt", None, None),
            P("space", "filt", None, None),
            P("filt", None, None),
            P("filt"),
            P("filt", None, None),
            P("filt"),
        ),
        check_vma=False,
    )
```

```python
import math

import jax
import jax.numpy as jnp
from jax import lax
from jax.experimental import pallas as pl
from jax.experimental.pallas import tpu as pltpu
from jax.sharding import PartitionSpec as P

F32 = jnp.float32
BF16 = jnp.bfloat16
TAP_PLACE = ((1, 1), (0, 0), (1, 0), (0, -1))
LANE = 128
PLANE = 1024
NEAR = 8


def vmem_call(body, outs, scratch=(), specs=None, limit=24 * 1024 * 1024):
    return pl.pallas_call(
        body,
        out_shape=outs,
        **({} if specs is None else {"in_specs": specs}),
        scratch_shapes=list(scratch),
        compiler_params=pltpu.CompilerParams(vmem_limit_bytes=limit),
    )


def ahead(value, step):
    extent = value.shape[-1]
    return value if step == 0 else pltpu.roll(value, (-step) % extent, value.ndim - 1)


def dot(a, b, dims=((1,), (0,))):
    return lax.dot_general(a, b, (dims, ((), ())), preferred_element_type=F32)


def hidden_kernel(odd, weight, pair, outer, bias, source, out, taps):
    @pl.when(odd[0] == 0)
    def _():
        source[:, :256] = outer[...]
        source[:, 256:512] = pair[:256]
        source[:, 512:] = pair[256:]

    @pl.when(odd[0] == 1)
    def _():
        source[:, :256] = pair[:256]
        source[:, 256:512] = pair[256:]
        source[:, 512:] = outer[...]

    taps[...] = dot(weight[...], source[...])

    def tap(kz, kx, ky, plane, xi):
        row = (kz * 16 + kx * 4 + ky) * 8
        col = plane * 256 + xi * LANE
        return taps[row : row + 8, col : col + LANE]

    for plane in range(4):
        parity_z = (plane + 1) % 2
        base_z = (plane + 1) // 2
        along_z = [(k, base_z + off) for k, (par, off) in enumerate(TAP_PLACE) if par == parity_z]
        for x in range(4):
            along_x = [
                (k, (x // 2 + off) % 2) for k, (par, off) in enumerate(TAP_PLACE) if par == x % 2
            ]
            for parity_y in range(2):
                total = bias[...]
                for ky, (par, off) in enumerate(TAP_PLACE):
                    if par != parity_y:
                        continue
                    part = None
                    for kz, iz in along_z:
                        for kx, ix in along_x:
                            term = tap(kz, kx, ky, iz, ix)
                            part = term if part is None else part + term
                    total = total + ahead(part, off)
                col = plane * PLANE + x * 256 + parity_y * LANE
                value = total.astype(BF16)
                for copy in range(out.shape[0]):
                    out[copy, :, col : col + LANE] = value


def copies_kernel(field, out):
    rows = field[...].astype(F32)
    plane = jnp.concatenate([rows[:, 0, :], rows[:, 1, :]], axis=1).astype(BF16)
    for i in range(out.shape[0]):
        out[i] = plane


def spread_rows(rows, cols):
    natural = lax.broadcasted_iota(jnp.int32, (rows, cols), 0)
    split = lax.broadcasted_iota(jnp.int32, (rows, cols), 1)
    return jnp.where(natural == 2 * (split % LANE) + split // LANE, 1.0, 0.0).astype(BF16)


def split_kernel(field, out, rows):
    rows[...] = dot(field[...], spread_rows(256, 256))
    for z in range(2):
        for x in range(4):
            col = z * PLANE + x * 256
            for e in range(8):
                line = z * 32 + e * 4 + x
                out[e : e + 1, col : col + 256] = rows[line : line + 1, :]


def activate_kernel(
    near, across, weight, bias, cot, turned, active, share, dpre, moved, taps, cols
):
    hidden = jnp.concatenate([near[...], across[...]], axis=0)
    taps[...] = dot(weight[...], hidden)

    def column(plane, x, parity):
        return plane * PLANE + (x % 4) * 256 + parity * LANE

    for z in range(2):
        for x in range(4):
            for parity in range(2):
                pre = bias[...]
                for ty in (-1, 0, 1):
                    other = (parity + ty) % 2
                    step = (parity + ty) // 2
                    part = None
                    for tz in range(3):
                        for tx in range(3):
                            row = (tz * 9 + tx * 3 + ty + 1) * 8
                            col = column(z + tz, x + tx - 1, other)
                            term = taps[row : row + 8, col : col + LANE]
                            part = term if part is None else part + term
                    pre = pre + ahead(part, step)
                sigma = 1.0 / (1.0 + jnp.exp(-pre))
                col = column(z, x, parity)
                active[:, col : col + LANE] = pre * sigma
                slope = cot[:, col : col + LANE] * sigma * (1.0 + pre * (1.0 - sigma))
                dpre[:, col : col + LANE] = slope.astype(BF16).astype(F32)

    for z in range(2):
        cols[z * LANE + 72 : (z + 1) * LANE, :] = jnp.zeros((LANE - 72, PLANE), F32)
        for x in range(4):
            for parity in range(2):
                for ty in (-1, 0, 1):
                    other = (parity - ty) % 2
                    step = (parity - ty) // 2
                    for tx in range(3):
                        col = column(z, x - (tx - 1), other)
                        value = ahead(dpre[:, col : col + LANE], step)
                        row = z * LANE + (tx * 3 + ty + 1) * 8
                        col = column(0, x, parity)
                        cols[row : row + 8, col : col + LANE] = value
    moved[...] = cols[...].astype(BF16)
    channel_sums(turned, moved, slice(64, 128), share)


def channel_sums(turned, moved, rows, out):
    out[:, :PLANE] = dot(turned[rows, 2 * LANE :], moved[:LANE]).astype(BF16)
    out[:, PLANE : 2 * PLANE] = dot(turned[rows, LANE:], moved[...]).astype(BF16)
    out[:, 2 * PLANE : 3 * PLANE] = dot(turned[rows, : 2 * LANE], moved[...]).astype(BF16)
    out[:, 3 * PLANE :] = dot(turned[rows, :LANE], moved[LANE:]).astype(BF16)


def mix_back_kernel(near, across, turned, active, dpre, moved, own, raw, result, rows):
    channel_sums(turned, moved, slice(0, 64), own)
    for z in range(2):
        for x in range(4):
            col = z * PLANE + x * 256
            both = active[:, col : col + 256].astype(BF16)
            natural = dot(both, spread_rows(256, 256), ((1,), (1,)))
            for e in range(8):
                line = z * 32 + e * 4 + x
                rows[line : line + 1, :] = natural[e : e + 1, :]
    for z in range(2):
        for e in range(8):
            line = z * 32 + e * 4
            result[z, e] = rows[line : line + 4, :].astype(BF16)
    for tz in range(3):
        for block, columns in ((near, slice(0, 64)), (across, slice(64, 128))):
            one = dot(moved[:LANE], block[:, tz * PLANE : (tz + 1) * PLANE], ((1,), (1,)))
            two = dot(moved[LANE:], block[:, (tz + 1) * PLANE : (tz + 2) * PLANE], ((1,), (1,)))
            raw[tz * 72 : (tz + 1) * 72, columns] = (one + two)[:72]
    total = jnp.sum(dpre[...], axis=1, keepdims=True)
    raw[216:224, :] = jnp.broadcast_to(total, (8, LANE))
    raw[224:256, :] = jnp.zeros((32, LANE), F32)


def pick_columns(field, out, base):
    for kx in range(4):
        for ky in range(4):
            parity, step = (ky - 1) % 2, (ky - 1) // 2
            for xi in range(2):
                x = (2 * xi - 1 + kx) % 4
                col = x * 256 + parity * LANE
                row = base + (kx * 4 + ky) * 8
                out[row : row + 8, xi * LANE : (xi + 1) * LANE] = ahead(
                    field[:, col : col + LANE], step
                )


def lift_back_kernel(parts, source, raw_second, low, high, message, cols, raw, second):
    total = parts[0].astype(F32)
    for f in range(1, parts.shape[0]):
        total = total + parts[f].astype(F32)
    low[...] = total[:, : 2 * PLANE]
    high[...] = total[:, 2 * PLANE :]
    for plane in range(4):
        pick_columns(total[:, plane * PLANE : (plane + 1) * PLANE], cols, plane * LANE)
    pairs = (((0, 1), (2, 2)), ((1, 1), (3, 2)), ((0, 0), (2, 1)), ((1, 0), (3, 1)))
    for kz, met in enumerate(pairs):
        part = None
        for plane, place in met:
            term = dot(
                cols[plane * LANE : (plane + 1) * LANE, :].astype(BF16),
                source[:, place * 256 : (place + 1) * 256],
                ((1,), (1,)),
            )
            part = term if part is None else part + term
        raw[kz * LANE : (kz + 1) * LANE, :] = part
    second[...] = raw_second[...]
    sums = (second[216:224, :], jnp.broadcast_to(jnp.sum(total, axis=1, keepdims=True), (8, LANE)))
    for i, value in enumerate(sums):
        high = value.astype(BF16).astype(F32)
        second[216 + 16 * i : 224 + 16 * i, :] = high
        second[224 + 16 * i : 232 + 16 * i, :] = value - high
    for i in range(NEAR):
        block = raw[64 * i : 64 * (i + 1), :].astype(BF16)
        message[i, 0:64, :] = block[:, :LANE]
        message[i, 64:128, :] = block[:, LANE:]
        message[i, 128:160, :] = second[32 * i : 32 * (i + 1), :].astype(BF16)


def lift_input_kernel(low, low_other, high, high_other, weight, share, cols):
    for half, (one, other) in enumerate(((low, low_other), (high, high_other))):
        total = (one[...] + other[...]).astype(BF16).astype(F32)
        pick_columns(total[:, :PLANE], cols, 2 * half * LANE)
        pick_columns(total[:, PLANE:], cols, (2 * half + 1) * LANE)
    share[...] = dot(weight[...], cols[...].astype(BF16)).astype(BF16)


def sum_kernel(parts, out):
    total = parts[0].astype(F32)
    for i in range(1, parts.shape[0]):
        total = total + parts[i].astype(F32)
    out[...] = total.astype(out.dtype)


def plane_kernel(parts, out):
    total = parts[0].astype(F32)
    for i in range(1, parts.shape[0]):
        total = total + parts[i].astype(F32)
    out[:, 0, :] = total[:, :LANE].astype(BF16)
    out[:, 1, :] = total[:, LANE:].astype(BF16)


def pair_kernel(one, other, out):
    total = (one[...].astype(F32) + other[...].astype(F32)).astype(BF16)
    out[...] = jnp.broadcast_to(total, out.shape)


def as_row(column):
    here = lax.broadcasted_iota(jnp.int32, (8, LANE), 0)
    lane = lax.broadcasted_iota(jnp.int32, (8, LANE), 1)
    return jnp.sum(jnp.where(here == lane, column, 0.0), axis=0, keepdims=True)[:, :8]


def finish_kernel(scale, parts, order, first, second, first_bias, second_bias, left, right, rest):
    for i in range(NEAR):
        left[64 * i : 64 * (i + 1), :] = parts[i, 0:64, :].astype(F32) * scale
        right[64 * i : 64 * (i + 1), :] = parts[i, 64:128, :].astype(F32) * scale
        rest[32 * i : 32 * (i + 1), :] = parts[i, 128:160, :].astype(F32)
    for d in range(8):
        first[d, :, :LANE] = left[pl.ds(d, 64, stride=8), :]
        first[d, :, LANE:] = right[pl.ds(d, 64, stride=8), :]
    second[...] = dot(rest[...].astype(BF16), order[...])[0:216] * scale
    second_bias[...] = as_row(rest[216:224, :] + rest[224:232, :]) * scale
    first_bias[...] = as_row(rest[232:240, :] + rest[240:248, :]) * scale


def shifted(value, step):
    count = lax.axis_size("space")
    return lax.ppermute(value, "space", [(i, (i + step) % count) for i in range(count)])


def chip_exchange(value):
    count = lax.axis_size("filt")
    groups = [list(range(core, count, 2)) for core in range(2)]
    return lax.all_to_all(value, "filt", 0, 0, axis_index_groups=groups, tiled=True)


def other_core(value):
    count = lax.axis_size("filt")
    return lax.ppermute(value, "filt", [(i, i ^ 1) for i in range(count)])


def pair_gather(copies):
    slabs, blocks = lax.axis_size("space"), lax.axis_size("filt")
    groups = [
        [s * blocks + f for s in (low, low + 1) for f in range(blocks)] for low in range(0, slabs, 2)
    ]
    return lax.all_to_all(copies, ("space", "filt"), 0, 0, axis_index_groups=groups, tiled=True)


def outer_plane(value):
    count = lax.axis_size("space")
    pairs = [(i, (((i + 1) ^ 1) - 1) % count) for i in range(count)]
    return lax.ppermute(value, "space", pairs)


def by_core(weight, core):
    split = weight.reshape(weight.shape[:-1] + (8, 2, 8))
    split = jnp.where(core == 0, split, jnp.flip(split, -2))
    return jnp.swapaxes(split, -3, -2).reshape(weight.shape)


def partner(value, ends):
    count = lax.axis_size("space")
    groups = count // NEAR
    pairs = []
    for i in range(count):
        group = i // NEAR
        other = ((group + ends) ^ 1) - ends
        pairs.append((i, other % groups * NEAR + i % NEAR))
    return lax.ppermute(value, "space", pairs)


def near_exchange(value):
    count = lax.axis_size("space")
    groups = [[g + i for i in range(NEAR)] for g in range(0, count, NEAR)]
    return lax.all_to_all(value, "space", 0, 0, axis_index_groups=groups, tiled=True)


def per_device(volume, first_weight, first_bias, second_weight, second_bias, cotangent):
    struct = jax.ShapeDtypeStruct
    wide = lambda bias: jnp.broadcast_to(bias.astype(F32)[:, None], (8, LANE))
    core = lax.axis_index("filt") % 2
    odd = lax.axis_index("space") % 2
    first_rows = first_weight.transpose(1, 0, 2).reshape(512, 256)
    first_turned = first_weight.transpose(2, 1, 0).reshape(256, 512)
    second = by_core(second_weight, core)
    second_rows = second.transpose(1, 0, 2).reshape(216, LANE)
    second_rows = jnp.pad(second_rows, ((0, 8), (0, 0)))
    second_turned = second.transpose(2, 1, 0).reshape(LANE, 3, 72)[:, ::-1]
    second_turned = jnp.pad(second_turned, ((0, 0), (0, 0), (0, 56))).reshape(LANE, 384)
    order = by_core(jnp.eye(LANE, dtype=BF16), core).T

    copies = vmem_call(copies_kernel, struct((32, 16, 256), BF16))(volume.reshape(16, 2, LANE))
    pair = pair_gather(copies).reshape(2, 256, 256)
    cot = vmem_call(
        split_kernel, struct((8, 2 * PLANE), F32), [pltpu.VMEM((64, 256), F32)]
    )(cotangent.reshape(64, 256))
    ready = (first_rows, first_turned, second_rows, second_turned, order)
    ready += (wide(first_bias), wide(second_bias), cot)
    pair, ready = lax.optimization_barrier((pair, ready))
    first_rows, first_turned, second_rows, second_turned, order = ready[:5]
    first_wide, second_wide, cot = ready[5:]
    outer = outer_plane(lax.dynamic_index_in_dim(pair, odd, 0, keepdims=False))
    whole = pl.BlockSpec(memory_space=pltpu.VMEM)
    source, hidden = vmem_call(
        hidden_kernel,
        (struct((256, 768), BF16), struct((8, 8, 4 * PLANE), BF16)),
        [pltpu.VMEM((512, 768), F32)],
        [pl.BlockSpec(memory_space=pltpu.SMEM)] + [whole] * 4,
    )(odd.reshape(1), first_rows, pair.reshape(512, 256), outer, first_wide)
    hidden = chip_exchange(hidden).reshape(64, 4 * PLANE)

    across = other_core(hidden)
    active, share, dpre, moved = vmem_call(
        activate_kernel,
        (
            struct((8, 2 * PLANE), F32),
            struct((64, 4 * PLANE), BF16),
            struct((8, 2 * PLANE), F32),
            struct((256, PLANE), BF16),
        ),
        [pltpu.VMEM((224, 4 * PLANE), F32), pltpu.VMEM((256, PLANE), F32)],
    )(hidden, across, second_rows, second_wide, cot, second_turned)
    own, raw_second, result = vmem_call(
        mix_back_kernel,
        (
            struct((64, 4 * PLANE), BF16),
            struct((256, LANE), F32),
            struct((2, 8, 4, 256), BF16),
        ),
        [pltpu.VMEM((64, 256), F32)],
    )(hidden, across, second_turned, active, dpre, moved)
    share = vmem_call(pair_kernel, struct((64, 4 * PLANE), BF16))(own, other_core(share))
    parts = chip_exchange(share.reshape(8, 8, 4 * PLANE))

    low, high, message = vmem_call(
        lift_back_kernel,
        (
            struct((8, 2 * PLANE), F32),
            struct((8, 2 * PLANE), F32),
            struct((NEAR, 160, LANE), BF16),
        ),
        [pltpu.VMEM((512, 256), F32), pltpu.VMEM((512, 256), F32), pltpu.VMEM((256, LANE), F32)],
    )(parts, source, raw_second)

    low_other = shifted(high, 1)
    high_other = shifted(low, -1)
    message = near_exchange(message)
    message, low_other, high_other = lax.optimization_barrier((message, low_other, high_other))
    share = vmem_call(
        lift_input_kernel, struct((256, 256), BF16), [pltpu.VMEM((512, 256), F32)]
    )(low, low_other, high, high_other, first_turned)
    mine = vmem_call(sum_kernel, struct((160, LANE), BF16))(message)
    share, mine = lax.optimization_barrier((share, mine))
    other = partner(mine, 0)
    share = lax.all_to_all(share.reshape(16, 16, 256), "filt", 0, 0, tiled=True)
    other, share = lax.optimization_barrier((other, share))
    mine = vmem_call(pair_kernel, struct((160, LANE), BF16))(mine, other)
    other = partner(mine, 1)
    message = vmem_call(pair_kernel, struct((NEAR, 160, LANE), BF16))(mine, other)
    message = near_exchange(message)
    grad_volume = vmem_call(plane_kernel, struct((16, 2, LANE), BF16))(share)

    total_cells = volume.shape[0] * lax.axis_size("space") * 8 * volume.shape[2] * volume.shape[3]
    scale = 1.0 / math.sqrt(total_cells)
    first, second, sum_first, sum_second = vmem_call(
        lambda *refs: finish_kernel(scale, *refs),
        (
            struct((8, 64, 256), F32),
            struct((216, LANE), F32),
            struct((1, 8), F32),
            struct((1, 8), F32),
        ),
        [pltpu.VMEM((520, LANE), F32), pltpu.VMEM((520, LANE), F32), pltpu.VMEM((256, LANE), F32)],
    )(message, order)
    return (
        result,
        grad_volume.reshape(1, 16, 2, 128),
        first,
        sum_first.reshape(8),
        second.reshape(27, 8, LANE).transpose(1, 0, 2),
        sum_second.reshape(8),
    )


def solution(mesh):
    placed = (
        P("space", "filt", None, None),
        P("filt", None, None),
        P("filt"),
        P("filt", None, None),
        P("filt"),
        P("space", "filt", None, None),
    )
    return jax.shard_map(
        per_device,
        mesh=mesh,
        in_specs=placed,
        out_specs=(
            P("space", "filt", None, None),
            P("space", "filt", None, None),
            P("filt", None, None),
            P("filt"),
            P("filt", None, None),
            P("filt"),
        ),
        check_vma=False,
    )
```

```python
import math

import jax
import jax.numpy as jnp
from jax import lax
from jax.experimental import pallas as pl
from jax.experimental.pallas import tpu as pltpu
from jax.sharding import PartitionSpec as P

F32 = jnp.float32
BF16 = jnp.bfloat16
TAP_PLACE = ((1, 1), (0, 0), (1, 0), (0, -1))
LANE = 128
PLANE = 1024
NEAR = 8


def vmem_call(body, outs, scratch=(), specs=None, limit=24 * 1024 * 1024):
    return pl.pallas_call(
        body,
        out_shape=outs,
        **({} if specs is None else {"in_specs": specs}),
        scratch_shapes=list(scratch),
        compiler_params=pltpu.CompilerParams(vmem_limit_bytes=limit),
    )


def ahead(value, step):
    extent = value.shape[-1]
    return value if step == 0 else pltpu.roll(value, (-step) % extent, value.ndim - 1)


def dot(a, b, dims=((1,), (0,))):
    return lax.dot_general(a, b, (dims, ((), ())), preferred_element_type=F32)


def hidden_kernel(odd, weight, pair, outer, bias, source, out, taps):
    @pl.when(odd[0] == 0)
    def _():
        source[:, :256] = outer[...]
        source[:, 256:512] = pair[:256]
        source[:, 512:] = pair[256:]

    @pl.when(odd[0] == 1)
    def _():
        source[:, :256] = pair[:256]
        source[:, 256:512] = pair[256:]
        source[:, 512:] = outer[...]

    taps[...] = dot(weight[...], source[...])

    def tap(kz, kx, ky, plane, xi):
        row = (kz * 16 + kx * 4 + ky) * 8
        col = plane * 256 + xi * LANE
        return taps[row : row + 8, col : col + LANE]

    for plane in range(4):
        parity_z = (plane + 1) % 2
        base_z = (plane + 1) // 2
        along_z = [(k, base_z + off) for k, (par, off) in enumerate(TAP_PLACE) if par == parity_z]
        for x in range(4):
            along_x = [
                (k, (x // 2 + off) % 2) for k, (par, off) in enumerate(TAP_PLACE) if par == x % 2
            ]
            for parity_y in range(2):
                total = bias[...]
                for ky, (par, off) in enumerate(TAP_PLACE):
                    if par != parity_y:
                        continue
                    part = None
                    for kz, iz in along_z:
                        for kx, ix in along_x:
                            term = tap(kz, kx, ky, iz, ix)
                            part = term if part is None else part + term
                    total = total + ahead(part, off)
                col = plane * PLANE + x * 256 + parity_y * LANE
                value = total.astype(BF16)
                for copy in range(out.shape[0]):
                    out[copy, :, col : col + LANE] = value


def copies_kernel(field, out):
    rows = field[...].astype(F32)
    plane = jnp.concatenate([rows[:, 0, :], rows[:, 1, :]], axis=1).astype(BF16)
    for i in range(out.shape[0]):
        out[i] = plane


def spread_rows(rows, cols):
    natural = lax.broadcasted_iota(jnp.int32, (rows, cols), 0)
    split = lax.broadcasted_iota(jnp.int32, (rows, cols), 1)
    return jnp.where(natural == 2 * (split % LANE) + split // LANE, 1.0, 0.0).astype(BF16)


def split_kernel(field, out, rows):
    rows[...] = dot(field[...], spread_rows(256, 256))
    for z in range(2):
        for x in range(4):
            col = z * PLANE + x * 256
            for e in range(8):
                line = z * 32 + e * 4 + x
                out[e : e + 1, col : col + 256] = rows[line : line + 1, :]


def activate_kernel(
    near, across, weight, bias, cot, turned, active, share, dpre, moved, taps, cols
):
    hidden = jnp.concatenate([near[...], across[...]], axis=0)
    taps[...] = dot(weight[...], hidden)

    def column(plane, x, parity):
        return plane * PLANE + (x % 4) * 256 + parity * LANE

    for z in range(2):
        for x in range(4):
            for parity in range(2):
                pre = bias[...]
                for ty in (-1, 0, 1):
                    other = (parity + ty) % 2
                    step = (parity + ty) // 2
                    part = None
                    for tz in range(3):
                        for tx in range(3):
                            row = (tz * 9 + tx * 3 + ty + 1) * 8
                            col = column(z + tz, x + tx - 1, other)
                            term = taps[row : row + 8, col : col + LANE]
                            part = term if part is None else part + term
                    pre = pre + ahead(part, step)
                sigma = 1.0 / (1.0 + jnp.exp(-pre))
                col = column(z, x, parity)
                active[:, col : col + LANE] = pre * sigma
                slope = cot[:, col : col + LANE] * sigma * (1.0 + pre * (1.0 - sigma))
                dpre[:, col : col + LANE] = slope.astype(BF16).astype(F32)

    for z in range(2):
        cols[z * LANE + 72 : (z + 1) * LANE, :] = jnp.zeros((LANE - 72, PLANE), F32)
        for x in range(4):
            for parity in range(2):
                for ty in (-1, 0, 1):
                    other = (parity - ty) % 2
                    step = (parity - ty) // 2
                    for tx in range(3):
                        col = column(z, x - (tx - 1), other)
                        value = ahead(dpre[:, col : col + LANE], step)
                        row = z * LANE + (tx * 3 + ty + 1) * 8
                        col = column(0, x, parity)
                        cols[row : row + 8, col : col + LANE] = value
    moved[...] = cols[...].astype(BF16)
    channel_sums(turned, moved, slice(64, 128), share)


def channel_sums(turned, moved, rows, out):
    out[:, :PLANE] = dot(turned[rows, 2 * LANE :], moved[:LANE]).astype(BF16)
    out[:, PLANE : 2 * PLANE] = dot(turned[rows, LANE:], moved[...]).astype(BF16)
    out[:, 2 * PLANE : 3 * PLANE] = dot(turned[rows, : 2 * LANE], moved[...]).astype(BF16)
    out[:, 3 * PLANE :] = dot(turned[rows, :LANE], moved[LANE:]).astype(BF16)


def result_kernel(active, result, rows):
    for z in range(2):
        for x in range(4):
            col = z * PLANE + x * 256
            both = active[:, col : col + 256].astype(BF16)
            natural = dot(both, spread_rows(256, 256), ((1,), (1,)))
            for e in range(8):
                line = z * 32 + e * 4 + x
                rows[line : line + 1, :] = natural[e : e + 1, :]
    for z in range(2):
        for e in range(8):
            line = z * 32 + e * 4
            result[z, e] = rows[line : line + 4, :].astype(BF16)


def mix_back_kernel(near, across, turned, dpre, moved, own, raw):
    channel_sums(turned, moved, slice(0, 64), own)
    for tz in range(3):
        for block, columns in ((near, slice(0, 64)), (across, slice(64, 128))):
            one = dot(moved[:LANE], block[:, tz * PLANE : (tz + 1) * PLANE], ((1,), (1,)))
            two = dot(moved[LANE:], block[:, (tz + 1) * PLANE : (tz + 2) * PLANE], ((1,), (1,)))
            raw[tz * 72 : (tz + 1) * 72, columns] = (one + two)[:72]
    total = jnp.sum(dpre[...], axis=1, keepdims=True)
    raw[216:224, :] = jnp.broadcast_to(total, (8, LANE))
    raw[224:256, :] = jnp.zeros((32, LANE), F32)


def pick_columns(field, out, base):
    for kx in range(4):
        for ky in range(4):
            parity, step = (ky - 1) % 2, (ky - 1) // 2
            for xi in range(2):
                x = (2 * xi - 1 + kx) % 4
                col = x * 256 + parity * LANE
                row = base + (kx * 4 + ky) * 8
                out[row : row + 8, xi * LANE : (xi + 1) * LANE] = ahead(
                    field[:, col : col + LANE], step
                )


def lift_back_kernel(parts, source, raw_second, low, high, message, cols, raw, second):
    total = parts[0].astype(F32)
    for f in range(1, parts.shape[0]):
        total = total + parts[f].astype(F32)
    low[...] = total[:, : 2 * PLANE].astype(BF16)
    high[...] = total[:, 2 * PLANE :].astype(BF16)
    for plane in range(4):
        pick_columns(total[:, plane * PLANE : (plane + 1) * PLANE], cols, plane * LANE)
    pairs = (((0, 1), (2, 2)), ((1, 1), (3, 2)), ((0, 0), (2, 1)), ((1, 0), (3, 1)))
    for kz, met in enumerate(pairs):
        part = None
        for plane, place in met:
            term = dot(
                cols[plane * LANE : (plane + 1) * LANE, :].astype(BF16),
                source[:, place * 256 : (place + 1) * 256],
                ((1,), (1,)),
            )
            part = term if part is None else part + term
        raw[kz * LANE : (kz + 1) * LANE, :] = part
    second[...] = raw_second[...]
    sums = (second[216:224, :], jnp.broadcast_to(jnp.sum(total, axis=1, keepdims=True), (8, LANE)))
    for i, value in enumerate(sums):
        high = value.astype(BF16).astype(F32)
        second[216 + 16 * i : 224 + 16 * i, :] = high
        second[224 + 16 * i : 232 + 16 * i, :] = value - high
    for i in range(NEAR):
        block = raw[64 * i : 64 * (i + 1), :].astype(BF16)
        message[i, 0:64, :] = block[:, :LANE]
        message[i, 64:128, :] = block[:, LANE:]
        message[i, 128:160, :] = second[32 * i : 32 * (i + 1), :].astype(BF16)


def lift_input_kernel(low, low_other, high, high_other, weight, share, cols):
    for half, (one, other) in enumerate(((low, low_other), (high, high_other))):
        total = (one[...].astype(F32) + other[...].astype(F32)).astype(BF16).astype(F32)
        pick_columns(total[:, :PLANE], cols, 2 * half * LANE)
        pick_columns(total[:, PLANE:], cols, (2 * half + 1) * LANE)
    share[...] = dot(weight[...], cols[...].astype(BF16)).astype(BF16)


def sum_kernel(parts, out):
    total = parts[0].astype(F32)
    for i in range(1, parts.shape[0]):
        total = total + parts[i].astype(F32)
    out[...] = total.astype(out.dtype)


def plane_kernel(parts, out):
    total = parts[0].astype(F32)
    for i in range(1, parts.shape[0]):
        total = total + parts[i].astype(F32)
    out[:, 0, :] = total[:, :LANE].astype(BF16)
    out[:, 1, :] = total[:, LANE:].astype(BF16)


def pair_kernel(one, other, out):
    total = (one[...].astype(F32) + other[...].astype(F32)).astype(BF16)
    out[...] = jnp.broadcast_to(total, out.shape)


def as_row(column):
    here = lax.broadcasted_iota(jnp.int32, (8, LANE), 0)
    lane = lax.broadcasted_iota(jnp.int32, (8, LANE), 1)
    return jnp.sum(jnp.where(here == lane, column, 0.0), axis=0, keepdims=True)[:, :8]


def finish_kernel(scale, parts, order, first, second, first_bias, second_bias, left, right, rest):
    for i in range(NEAR):
        left[64 * i : 64 * (i + 1), :] = parts[i, 0:64, :].astype(F32) * scale
        right[64 * i : 64 * (i + 1), :] = parts[i, 64:128, :].astype(F32) * scale
        rest[32 * i : 32 * (i + 1), :] = parts[i, 128:160, :].astype(F32)
    for d in range(8):
        first[d, :, :LANE] = left[pl.ds(d, 64, stride=8), :]
        first[d, :, LANE:] = right[pl.ds(d, 64, stride=8), :]
    second[...] = dot(rest[...].astype(BF16), order[...])[0:216] * scale
    second_bias[...] = as_row(rest[216:224, :] + rest[224:232, :]) * scale
    first_bias[...] = as_row(rest[232:240, :] + rest[240:248, :]) * scale


def shifted(value, step):
    count = lax.axis_size("space")
    return lax.ppermute(value, "space", [(i, (i + step) % count) for i in range(count)])


def chip_exchange(value):
    count = lax.axis_size("filt")
    groups = [list(range(core, count, 2)) for core in range(2)]
    return lax.all_to_all(value, "filt", 0, 0, axis_index_groups=groups, tiled=True)


def other_core(value):
    count = lax.axis_size("filt")
    return lax.ppermute(value, "filt", [(i, i ^ 1) for i in range(count)])


def pair_gather(copies):
    slabs, blocks = lax.axis_size("space"), lax.axis_size("filt")
    groups = [
        [s * blocks + f for s in (low, low + 1) for f in range(blocks)] for low in range(0, slabs, 2)
    ]
    return lax.all_to_all(copies, ("space", "filt"), 0, 0, axis_index_groups=groups, tiled=True)


def outer_plane(value):
    count = lax.axis_size("space")
    pairs = [(i, (((i + 1) ^ 1) - 1) % count) for i in range(count)]
    return lax.ppermute(value, "space", pairs)


def by_core(weight, core):
    split = weight.reshape(weight.shape[:-1] + (8, 2, 8))
    split = jnp.where(core == 0, split, jnp.flip(split, -2))
    return jnp.swapaxes(split, -3, -2).reshape(weight.shape)


def partner(value, ends):
    count = lax.axis_size("space")
    groups = count // NEAR
    pairs = []
    for i in range(count):
        group = i // NEAR
        other = ((group + ends) ^ 1) - ends
        pairs.append((i, other % groups * NEAR + i % NEAR))
    return lax.ppermute(value, "space", pairs)


def near_exchange(value):
    count = lax.axis_size("space")
    groups = [[g + i for i in range(NEAR)] for g in range(0, count, NEAR)]
    return lax.all_to_all(value, "space", 0, 0, axis_index_groups=groups, tiled=True)


def per_device(volume, first_weight, first_bias, second_weight, second_bias, cotangent):
    struct = jax.ShapeDtypeStruct
    wide = lambda bias: jnp.broadcast_to(bias.astype(F32)[:, None], (8, LANE))
    core = lax.axis_index("filt") % 2
    odd = lax.axis_index("space") % 2
    copies = vmem_call(copies_kernel, struct((32, 16, 256), BF16))(volume.reshape(16, 2, LANE))
    pair = pair_gather(copies).reshape(2, 256, 256)
    given = (first_weight, wide(first_bias), second_weight, wide(second_bias), cotangent)
    pair, given = lax.optimization_barrier((pair, given))
    first_weight, first_wide, second_weight, second_wide, cotangent = given
    first_rows = first_weight.transpose(1, 0, 2).reshape(512, 256)
    first_turned = first_weight.transpose(2, 1, 0).reshape(256, 512)
    second = by_core(second_weight, core)
    second_rows = second.transpose(1, 0, 2).reshape(216, LANE)
    second_rows = jnp.pad(second_rows, ((0, 8), (0, 0)))
    second_turned = second.transpose(2, 1, 0).reshape(LANE, 3, 72)[:, ::-1]
    second_turned = jnp.pad(second_turned, ((0, 0), (0, 0), (0, 56))).reshape(LANE, 384)
    order = by_core(jnp.eye(LANE, dtype=BF16), core).T
    cot = vmem_call(
        split_kernel, struct((8, 2 * PLANE), F32), [pltpu.VMEM((64, 256), F32)]
    )(cotangent.reshape(64, 256))
    outer = outer_plane(lax.dynamic_index_in_dim(pair, odd, 0, keepdims=False))
    ready = (first_rows, first_turned, second_rows, second_turned, order, cot)
    outer, ready = lax.optimization_barrier((outer, ready))
    first_rows, first_turned, second_rows, second_turned, order, cot = ready
    whole = pl.BlockSpec(memory_space=pltpu.VMEM)
    source, hidden = vmem_call(
        hidden_kernel,
        (struct((256, 768), BF16), struct((8, 8, 4 * PLANE), BF16)),
        [pltpu.VMEM((512, 768), F32)],
        [pl.BlockSpec(memory_space=pltpu.SMEM)] + [whole] * 4,
    )(odd.reshape(1), first_rows, pair.reshape(512, 256), outer, first_wide)
    hidden = chip_exchange(hidden).reshape(64, 4 * PLANE)

    across = other_core(hidden)
    active, share, dpre, moved = vmem_call(
        activate_kernel,
        (
            struct((8, 2 * PLANE), F32),
            struct((64, 4 * PLANE), BF16),
            struct((8, 2 * PLANE), F32),
            struct((256, PLANE), BF16),
        ),
        [pltpu.VMEM((224, 4 * PLANE), F32), pltpu.VMEM((256, PLANE), F32)],
    )(hidden, across, second_rows, second_wide, cot, second_turned)
    own, raw_second = vmem_call(
        mix_back_kernel, (struct((64, 4 * PLANE), BF16), struct((256, LANE), F32))
    )(hidden, across, second_turned, dpre, moved)
    share = vmem_call(pair_kernel, struct((64, 4 * PLANE), BF16))(own, other_core(share))
    parts = chip_exchange(share.reshape(8, 8, 4 * PLANE))

    low, high, message = vmem_call(
        lift_back_kernel,
        (
            struct((8, 2 * PLANE), BF16),
            struct((8, 2 * PLANE), BF16),
            struct((NEAR, 160, LANE), BF16),
        ),
        [pltpu.VMEM((512, 256), F32), pltpu.VMEM((512, 256), F32), pltpu.VMEM((256, LANE), F32)],
    )(parts, source, raw_second)

    low_other = shifted(high, 1)
    high_other = shifted(low, -1)
    message = near_exchange(message)
    result = vmem_call(
        result_kernel, struct((2, 8, 4, 256), BF16), [pltpu.VMEM((64, 256), F32)]
    )(active)
    message, low_other, high_other, result = lax.optimization_barrier(
        (message, low_other, high_other, result)
    )
    share = vmem_call(
        lift_input_kernel, struct((256, 256), BF16), [pltpu.VMEM((512, 256), F32)]
    )(low, low_other, high, high_other, first_turned)
    mine = vmem_call(sum_kernel, struct((160, LANE), BF16))(message)
    share, mine = lax.optimization_barrier((share, mine))
    other = partner(mine, 0)
    share = lax.all_to_all(share.reshape(16, 16, 256), "filt", 0, 0, tiled=True)
    other, share = lax.optimization_barrier((other, share))
    mine = vmem_call(pair_kernel, struct((160, LANE), BF16))(mine, other)
    other = partner(mine, 1)
    grad_volume = vmem_call(plane_kernel, struct((16, 2, LANE), BF16))(share)
    other, grad_volume = lax.optimization_barrier((other, grad_volume))
    message = vmem_call(pair_kernel, struct((NEAR, 160, LANE), BF16))(mine, other)
    message = near_exchange(message)

    total_cells = volume.shape[0] * lax.axis_size("space") * 8 * volume.shape[2] * volume.shape[3]
    scale = 1.0 / math.sqrt(total_cells)
    first, second, sum_first, sum_second = vmem_call(
        lambda *refs: finish_kernel(scale, *refs),
        (
            struct((8, 64, 256), F32),
            struct((216, LANE), F32),
            struct((1, 8), F32),
            struct((1, 8), F32),
        ),
        [pltpu.VMEM((520, LANE), F32), pltpu.VMEM((520, LANE), F32), pltpu.VMEM((256, LANE), F32)],
    )(message, order)
    return (
        result,
        grad_volume.reshape(1, 16, 2, 128),
        first,
        sum_first.reshape(8),
        second.reshape(27, 8, LANE).transpose(1, 0, 2),
        sum_second.reshape(8),
    )


def solution(mesh):
    placed = (
        P("space", "filt", None, None),
        P("filt", None, None),
        P("filt"),
        P("filt", None, None),
        P("filt"),
        P("space", "filt", None, None),
    )
    return jax.shard_map(
        per_device,
        mesh=mesh,
        in_specs=placed,
        out_specs=(
            P("space", "filt", None, None),
            P("space", "filt", None, None),
            P("filt", None, None),
            P("filt"),
            P("filt", None, None),
            P("filt"),
        ),
        check_vma=False,
    )
```

```python
import math

import jax
import jax.numpy as jnp
from jax import lax
from jax.experimental import pallas as pl
from jax.experimental.pallas import tpu as pltpu
from jax.sharding import PartitionSpec as P

F32 = jnp.float32
BF16 = jnp.bfloat16
TAP_PLACE = ((1, 1), (0, 0), (1, 0), (0, -1))
LANE = 128
PLANE = 1024
NEAR = 8


def vmem_call(body, outs, scratch=(), specs=None, limit=24 * 1024 * 1024):
    return pl.pallas_call(
        body,
        out_shape=outs,
        **({} if specs is None else {"in_specs": specs}),
        scratch_shapes=list(scratch),
        compiler_params=pltpu.CompilerParams(vmem_limit_bytes=limit),
    )


def ahead(value, step):
    extent = value.shape[-1]
    return value if step == 0 else pltpu.roll(value, (-step) % extent, value.ndim - 1)


def dot(a, b, dims=((1,), (0,))):
    return lax.dot_general(a, b, (dims, ((), ())), preferred_element_type=F32)


def hidden_kernel(odd, weight, pair, outer, bias, source, out, taps):
    @pl.when(odd[0] == 0)
    def _():
        source[:, :256] = outer[...]
        source[:, 256:512] = pair[:256]
        source[:, 512:] = pair[256:]

    @pl.when(odd[0] == 1)
    def _():
        source[:, :256] = pair[:256]
        source[:, 256:512] = pair[256:]
        source[:, 512:] = outer[...]

    taps[...] = dot(weight[...], source[...])

    def tap(kz, kx, ky, plane, xi):
        row = (kz * 16 + kx * 4 + ky) * 8
        col = plane * 256 + xi * LANE
        return taps[row : row + 8, col : col + LANE]

    for plane in range(4):
        parity_z = (plane + 1) % 2
        base_z = (plane + 1) // 2
        along_z = [(k, base_z + off) for k, (par, off) in enumerate(TAP_PLACE) if par == parity_z]
        for x in range(4):
            along_x = [
                (k, (x // 2 + off) % 2) for k, (par, off) in enumerate(TAP_PLACE) if par == x % 2
            ]
            for parity_y in range(2):
                total = bias[...]
                for ky, (par, off) in enumerate(TAP_PLACE):
                    if par != parity_y:
                        continue
                    part = None
                    for kz, iz in along_z:
                        for kx, ix in along_x:
                            term = tap(kz, kx, ky, iz, ix)
                            part = term if part is None else part + term
                    total = total + ahead(part, off)
                col = plane * PLANE + x * 256 + parity_y * LANE
                value = total.astype(BF16)
                for copy in range(out.shape[0]):
                    out[copy, :, col : col + LANE] = value


def copies_kernel(field, out):
    rows = field[...].astype(F32)
    plane = jnp.concatenate([rows[:, 0, :], rows[:, 1, :]], axis=1).astype(BF16)
    for i in range(out.shape[0]):
        out[i] = plane


def spread_rows(rows, cols):
    natural = lax.broadcasted_iota(jnp.int32, (rows, cols), 0)
    split = lax.broadcasted_iota(jnp.int32, (rows, cols), 1)
    return jnp.where(natural == 2 * (split % LANE) + split // LANE, 1.0, 0.0).astype(BF16)


def split_kernel(field, out, rows):
    rows[...] = dot(field[...], spread_rows(256, 256))
    for z in range(2):
        for x in range(4):
            col = z * PLANE + x * 256
            for e in range(8):
                line = z * 32 + e * 4 + x
                out[e : e + 1, col : col + 256] = rows[line : line + 1, :]


def activate_kernel(
    near, across, weight, bias, cot, turned, active, share, dpre, moved, taps, cols
):
    hidden = jnp.concatenate([near[...], across[...]], axis=0)
    taps[...] = dot(weight[...], hidden)

    def column(plane, x, parity):
        return plane * PLANE + (x % 4) * 256 + parity * LANE

    for z in range(2):
        for x in range(4):
            for parity in range(2):
                pre = bias[...]
                for ty in (-1, 0, 1):
                    other = (parity + ty) % 2
                    step = (parity + ty) // 2
                    part = None
                    for tz in range(3):
                        for tx in range(3):
                            row = (tz * 9 + tx * 3 + ty + 1) * 8
                            col = column(z + tz, x + tx - 1, other)
                            term = taps[row : row + 8, col : col + LANE]
                            part = term if part is None else part + term
                    pre = pre + ahead(part, step)
                sigma = 1.0 / (1.0 + jnp.exp(-pre))
                col = column(z, x, parity)
                active[:, col : col + LANE] = pre * sigma
                slope = cot[:, col : col + LANE] * sigma * (1.0 + pre * (1.0 - sigma))
                dpre[:, col : col + LANE] = slope.astype(BF16).astype(F32)

    for z in range(2):
        cols[z * LANE + 72 : (z + 1) * LANE, :] = jnp.zeros((LANE - 72, PLANE), F32)
        for x in range(4):
            for parity in range(2):
                for ty in (-1, 0, 1):
                    other = (parity - ty) % 2
                    step = (parity - ty) // 2
                    for tx in range(3):
                        col = column(z, x - (tx - 1), other)
                        value = ahead(dpre[:, col : col + LANE], step)
                        row = z * LANE + (tx * 3 + ty + 1) * 8
                        col = column(0, x, parity)
                        cols[row : row + 8, col : col + LANE] = value
    moved[...] = cols[...].astype(BF16)
    channel_sums(turned, moved, slice(64, 128), share)


def channel_sums(turned, moved, rows, out):
    out[:, :PLANE] = dot(turned[rows, 2 * LANE :], moved[:LANE]).astype(BF16)
    out[:, PLANE : 2 * PLANE] = dot(turned[rows, LANE:], moved[...]).astype(BF16)
    out[:, 2 * PLANE : 3 * PLANE] = dot(turned[rows, : 2 * LANE], moved[...]).astype(BF16)
    out[:, 3 * PLANE :] = dot(turned[rows, :LANE], moved[LANE:]).astype(BF16)


def result_kernel(active, result, rows):
    for z in range(2):
        for x in range(4):
            col = z * PLANE + x * 256
            both = active[:, col : col + 256].astype(BF16)
            natural = dot(both, spread_rows(256, 256), ((1,), (1,)))
            for e in range(8):
                line = z * 32 + e * 4 + x
                rows[line : line + 1, :] = natural[e : e + 1, :]
    for z in range(2):
        for e in range(8):
            line = z * 32 + e * 4
            result[z, e] = rows[line : line + 4, :].astype(BF16)


def mix_back_kernel(near, across, turned, dpre, moved, own, raw):
    channel_sums(turned, moved, slice(0, 64), own)
    for tz in range(3):
        for block, columns in ((near, slice(0, 64)), (across, slice(64, 128))):
            one = dot(moved[:LANE], block[:, tz * PLANE : (tz + 1) * PLANE], ((1,), (1,)))
            two = dot(moved[LANE:], block[:, (tz + 1) * PLANE : (tz + 2) * PLANE], ((1,), (1,)))
            raw[tz * 72 : (tz + 1) * 72, columns] = (one + two)[:72]
    total = jnp.sum(dpre[...], axis=1, keepdims=True)
    raw[216:224, :] = jnp.broadcast_to(total, (8, LANE))
    raw[224:256, :] = jnp.zeros((32, LANE), F32)


def pick_columns(field, out, base):
    for kx in range(4):
        for ky in range(4):
            parity, step = (ky - 1) % 2, (ky - 1) // 2
            for xi in range(2):
                x = (2 * xi - 1 + kx) % 4
                col = x * 256 + parity * LANE
                row = base + (kx * 4 + ky) * 8
                out[row : row + 8, xi * LANE : (xi + 1) * LANE] = ahead(
                    field[:, col : col + LANE], step
                )


def lift_back_kernel(parts, source, raw_second, low, high, message, cols, raw, second):
    total = parts[0].astype(F32)
    for f in range(1, parts.shape[0]):
        total = total + parts[f].astype(F32)
    low[...] = total[:, : 2 * PLANE].astype(BF16)
    high[...] = total[:, 2 * PLANE :].astype(BF16)
    for plane in range(4):
        pick_columns(total[:, plane * PLANE : (plane + 1) * PLANE], cols, plane * LANE)
    pairs = (((0, 1), (2, 2)), ((1, 1), (3, 2)), ((0, 0), (2, 1)), ((1, 0), (3, 1)))
    for kz, met in enumerate(pairs):
        part = None
        for plane, place in met:
            term = dot(
                cols[plane * LANE : (plane + 1) * LANE, :].astype(BF16),
                source[:, place * 256 : (place + 1) * 256],
                ((1,), (1,)),
            )
            part = term if part is None else part + term
        raw[kz * LANE : (kz + 1) * LANE, :] = part
    second[...] = raw_second[...]
    sums = (second[216:224, :], jnp.broadcast_to(jnp.sum(total, axis=1, keepdims=True), (8, LANE)))
    for i, value in enumerate(sums):
        high = value.astype(BF16).astype(F32)
        second[216 + 16 * i : 224 + 16 * i, :] = high
        second[224 + 16 * i : 232 + 16 * i, :] = value - high
    for i in range(NEAR):
        block = raw[64 * i : 64 * (i + 1), :].astype(BF16)
        message[i, 0:64, :] = block[:, :LANE]
        message[i, 64:128, :] = block[:, LANE:]
        message[i, 128:160, :] = second[32 * i : 32 * (i + 1), :].astype(BF16)


def lift_input_kernel(low, low_other, high, high_other, weight, share, cols):
    for half, (one, other) in enumerate(((low, low_other), (high, high_other))):
        total = (one[...].astype(F32) + other[...].astype(F32)).astype(BF16).astype(F32)
        pick_columns(total[:, :PLANE], cols, 2 * half * LANE)
        pick_columns(total[:, PLANE:], cols, (2 * half + 1) * LANE)
    share[...] = dot(weight[...], cols[...].astype(BF16)).astype(BF16)


def sum_kernel(parts, out):
    total = parts[0].astype(F32)
    for i in range(1, parts.shape[0]):
        total = total + parts[i].astype(F32)
    out[...] = total.astype(out.dtype)


def plane_kernel(parts, out):
    total = parts[0].astype(F32)
    for i in range(1, parts.shape[0]):
        total = total + parts[i].astype(F32)
    out[:, 0, :] = total[:, :LANE].astype(BF16)
    out[:, 1, :] = total[:, LANE:].astype(BF16)


def pair_kernel(one, other, out):
    total = (one[...].astype(F32) + other[...].astype(F32)).astype(BF16)
    out[...] = jnp.broadcast_to(total, out.shape)


def as_row(column):
    here = lax.broadcasted_iota(jnp.int32, (8, LANE), 0)
    lane = lax.broadcasted_iota(jnp.int32, (8, LANE), 1)
    return jnp.sum(jnp.where(here == lane, column, 0.0), axis=0, keepdims=True)[:, :8]


def finish_kernel(scale, parts, order, first, second, first_bias, second_bias, left, right, rest):
    for i in range(NEAR):
        left[64 * i : 64 * (i + 1), :] = parts[i, 0:64, :].astype(F32) * scale
        right[64 * i : 64 * (i + 1), :] = parts[i, 64:128, :].astype(F32) * scale
        rest[32 * i : 32 * (i + 1), :] = parts[i, 128:160, :].astype(F32)
    for d in range(8):
        first[d, :, :LANE] = left[pl.ds(d, 64, stride=8), :]
        first[d, :, LANE:] = right[pl.ds(d, 64, stride=8), :]
    second[...] = dot(rest[...].astype(BF16), order[...])[0:216] * scale
    second_bias[...] = as_row(rest[216:224, :] + rest[224:232, :]) * scale
    first_bias[...] = as_row(rest[232:240, :] + rest[240:248, :]) * scale


def shifted(value, step):
    count = lax.axis_size("space")
    return lax.ppermute(value, "space", [(i, (i + step) % count) for i in range(count)])


def chip_exchange(value):
    count = lax.axis_size("filt")
    groups = [list(range(core, count, 2)) for core in range(2)]
    return lax.all_to_all(value, "filt", 0, 0, axis_index_groups=groups, tiled=True)


def other_core(value):
    count = lax.axis_size("filt")
    return lax.ppermute(value, "filt", [(i, i ^ 1) for i in range(count)])


def pair_gather(copies):
    slabs, blocks = lax.axis_size("space"), lax.axis_size("filt")
    groups = [
        [s * blocks + f for s in (low, low + 1) for f in range(blocks)] for low in range(0, slabs, 2)
    ]
    return lax.all_to_all(copies, ("space", "filt"), 0, 0, axis_index_groups=groups, tiled=True)


def outer_plane(value):
    count = lax.axis_size("space")
    pairs = [(i, (((i + 1) ^ 1) - 1) % count) for i in range(count)]
    return lax.ppermute(value, "space", pairs)


def by_core(weight, core):
    split = weight.reshape(weight.shape[:-1] + (8, 2, 8))
    split = jnp.where(core == 0, split, jnp.flip(split, -2))
    return jnp.swapaxes(split, -3, -2).reshape(weight.shape)


def partner(value, turn):
    slabs, blocks = lax.axis_size("space"), lax.axis_size("filt")
    groups = slabs // NEAR
    pairs = []
    for s in range(slabs):
        for f in range(blocks):
            ends = (turn + f) % 2
            other = (((s // NEAR + ends) ^ 1) - ends) % groups * NEAR + s % NEAR
            pairs.append((s * blocks + f, other * blocks + f))
    return lax.ppermute(value, ("space", "filt"), pairs)


def near_exchange(value):
    count = lax.axis_size("space")
    groups = [[g + i for i in range(NEAR)] for g in range(0, count, NEAR)]
    return lax.all_to_all(value, "space", 0, 0, axis_index_groups=groups, tiled=True)


def per_device(volume, first_weight, first_bias, second_weight, second_bias, cotangent):
    struct = jax.ShapeDtypeStruct
    wide = lambda bias: jnp.broadcast_to(bias.astype(F32)[:, None], (8, LANE))
    core = lax.axis_index("filt") % 2
    odd = lax.axis_index("space") % 2
    copies = vmem_call(copies_kernel, struct((32, 16, 256), BF16))(volume.reshape(16, 2, LANE))
    pair = pair_gather(copies).reshape(2, 256, 256)
    given = (first_weight, wide(first_bias), second_weight, wide(second_bias), cotangent)
    pair, given = lax.optimization_barrier((pair, given))
    first_weight, first_wide, second_weight, second_wide, cotangent = given
    first_rows = first_weight.transpose(1, 0, 2).reshape(512, 256)
    first_turned = first_weight.transpose(2, 1, 0).reshape(256, 512)
    second = by_core(second_weight, core)
    second_rows = second.transpose(1, 0, 2).reshape(216, LANE)
    second_rows = jnp.pad(second_rows, ((0, 8), (0, 0)))
    second_turned = second.transpose(2, 1, 0).reshape(LANE, 3, 72)[:, ::-1]
    second_turned = jnp.pad(second_turned, ((0, 0), (0, 0), (0, 56))).reshape(LANE, 384)
    order = by_core(jnp.eye(LANE, dtype=BF16), core).T
    cot = vmem_call(
        split_kernel, struct((8, 2 * PLANE), F32), [pltpu.VMEM((64, 256), F32)]
    )(cotangent.reshape(64, 256))
    outer = outer_plane(lax.dynamic_index_in_dim(pair, odd, 0, keepdims=False))
    ready = (first_rows, first_turned, second_rows, second_turned, order, cot)
    outer, ready = lax.optimization_barrier((outer, ready))
    first_rows, first_turned, second_rows, second_turned, order, cot = ready
    whole = pl.BlockSpec(memory_space=pltpu.VMEM)
    source, hidden = vmem_call(
        hidden_kernel,
        (struct((256, 768), BF16), struct((8, 8, 4 * PLANE), BF16)),
        [pltpu.VMEM((512, 768), F32)],
        [pl.BlockSpec(memory_space=pltpu.SMEM)] + [whole] * 4,
    )(odd.reshape(1), first_rows, pair.reshape(512, 256), outer, first_wide)
    hidden = chip_exchange(hidden).reshape(64, 4 * PLANE)

    across = other_core(hidden)
    active, share, dpre, moved = vmem_call(
        activate_kernel,
        (
            struct((8, 2 * PLANE), F32),
            struct((64, 4 * PLANE), BF16),
            struct((8, 2 * PLANE), F32),
            struct((256, PLANE), BF16),
        ),
        [pltpu.VMEM((224, 4 * PLANE), F32), pltpu.VMEM((256, PLANE), F32)],
    )(hidden, across, second_rows, second_wide, cot, second_turned)
    own, raw_second = vmem_call(
        mix_back_kernel, (struct((64, 4 * PLANE), BF16), struct((256, LANE), F32))
    )(hidden, across, second_turned, dpre, moved)
    share = vmem_call(pair_kernel, struct((64, 4 * PLANE), BF16))(own, other_core(share))
    parts = chip_exchange(share.reshape(8, 8, 4 * PLANE))

    low, high, message = vmem_call(
        lift_back_kernel,
        (
            struct((8, 2 * PLANE), BF16),
            struct((8, 2 * PLANE), BF16),
            struct((NEAR, 160, LANE), BF16),
        ),
        [pltpu.VMEM((512, 256), F32), pltpu.VMEM((512, 256), F32), pltpu.VMEM((256, LANE), F32)],
    )(parts, source, raw_second)

    low_other = shifted(high, 1)
    high_other = shifted(low, -1)
    message = near_exchange(message)
    result = vmem_call(
        result_kernel, struct((2, 8, 4, 256), BF16), [pltpu.VMEM((64, 256), F32)]
    )(active)
    message, low_other, high_other, result = lax.optimization_barrier(
        (message, low_other, high_other, result)
    )
    share = vmem_call(
        lift_input_kernel, struct((256, 256), BF16), [pltpu.VMEM((512, 256), F32)]
    )(low, low_other, high, high_other, first_turned)
    mine = vmem_call(sum_kernel, struct((160, LANE), BF16))(message)
    share, mine = lax.optimization_barrier((share, mine))
    other = partner(mine, 0)
    share = lax.all_to_all(share.reshape(16, 16, 256), "filt", 0, 0, tiled=True)
    other, share = lax.optimization_barrier((other, share))
    mine = vmem_call(pair_kernel, struct((160, LANE), BF16))(mine, other)
    other = partner(mine, 1)
    grad_volume = vmem_call(plane_kernel, struct((16, 2, LANE), BF16))(share)
    other, grad_volume = lax.optimization_barrier((other, grad_volume))
    message = vmem_call(pair_kernel, struct((NEAR, 160, LANE), BF16))(mine, other)
    message = near_exchange(message)

    total_cells = volume.shape[0] * lax.axis_size("space") * 8 * volume.shape[2] * volume.shape[3]
    scale = 1.0 / math.sqrt(total_cells)
    first, second, sum_first, sum_second = vmem_call(
        lambda *refs: finish_kernel(scale, *refs),
        (
            struct((8, 64, 256), F32),
            struct((216, LANE), F32),
            struct((1, 8), F32),
            struct((1, 8), F32),
        ),
        [pltpu.VMEM((520, LANE), F32), pltpu.VMEM((520, LANE), F32), pltpu.VMEM((256, LANE), F32)],
    )(message, order)
    return (
        result,
        grad_volume.reshape(1, 16, 2, 128),
        first,
        sum_first.reshape(8),
        second.reshape(27, 8, LANE).transpose(1, 0, 2),
        sum_second.reshape(8),
    )


def solution(mesh):
    placed = (
        P("space", "filt", None, None),
        P("filt", None, None),
        P("filt"),
        P("filt", None, None),
        P("filt"),
        P("space", "filt", None, None),
    )
    return jax.shard_map(
        per_device,
        mesh=mesh,
        in_specs=placed,
        out_specs=(
            P("space", "filt", None, None),
            P("space", "filt", None, None),
            P("filt", None, None),
            P("filt"),
            P("filt", None, None),
            P("filt"),
        ),
        check_vma=False,
    )
```

```python
import math

import jax
import jax.numpy as jnp
from jax import lax
from jax.experimental import pallas as pl
from jax.experimental.pallas import tpu as pltpu
from jax.sharding import PartitionSpec as P

F32 = jnp.float32
BF16 = jnp.bfloat16
TAP_PLACE = ((1, 1), (0, 0), (1, 0), (0, -1))
LANE = 128
PLANE = 1024
NEAR = 8


def vmem_call(body, outs, scratch=(), specs=None, limit=24 * 1024 * 1024):
    return pl.pallas_call(
        body,
        out_shape=outs,
        **({} if specs is None else {"in_specs": specs}),
        scratch_shapes=list(scratch),
        compiler_params=pltpu.CompilerParams(vmem_limit_bytes=limit),
    )


def ahead(value, step):
    extent = value.shape[-1]
    return value if step == 0 else pltpu.roll(value, (-step) % extent, value.ndim - 1)


def dot(a, b, dims=((1,), (0,))):
    return lax.dot_general(a, b, (dims, ((), ())), preferred_element_type=F32)


def hidden_kernel(odd, weight, pair, outer, bias, source, out, taps):
    @pl.when(odd[0] == 0)
    def _():
        source[:, :256] = outer[...]
        source[:, 256:512] = pair[:256]
        source[:, 512:] = pair[256:]

    @pl.when(odd[0] == 1)
    def _():
        source[:, :256] = pair[:256]
        source[:, 256:512] = pair[256:]
        source[:, 512:] = outer[...]

    taps[...] = dot(weight[...], source[...])

    def tap(kz, kx, ky, plane, xi):
        row = (kz * 16 + kx * 4 + ky) * 8
        col = plane * 256 + xi * LANE
        return taps[row : row + 8, col : col + LANE]

    for plane in range(4):
        parity_z = (plane + 1) % 2
        base_z = (plane + 1) // 2
        along_z = [(k, base_z + off) for k, (par, off) in enumerate(TAP_PLACE) if par == parity_z]
        for x in range(4):
            along_x = [
                (k, (x // 2 + off) % 2) for k, (par, off) in enumerate(TAP_PLACE) if par == x % 2
            ]
            for parity_y in range(2):
                total = bias[...]
                for ky, (par, off) in enumerate(TAP_PLACE):
                    if par != parity_y:
                        continue
                    part = None
                    for kz, iz in along_z:
                        for kx, ix in along_x:
                            term = tap(kz, kx, ky, iz, ix)
                            part = term if part is None else part + term
                    total = total + ahead(part, off)
                col = plane * PLANE + x * 256 + parity_y * LANE
                value = total.astype(BF16)
                for copy in range(out.shape[0]):
                    out[copy, :, col : col + LANE] = value


def copies_kernel(field, out, local):
    pltpu.sync_copy(field, local)
    rows = local[...].astype(F32)
    plane = jnp.concatenate([rows[:, 0, :], rows[:, 1, :]], axis=1).astype(BF16)
    for i in range(out.shape[0]):
        out[i] = plane


def spread_rows(rows, cols):
    natural = lax.broadcasted_iota(jnp.int32, (rows, cols), 0)
    split = lax.broadcasted_iota(jnp.int32, (rows, cols), 1)
    return jnp.where(natural == 2 * (split % LANE) + split // LANE, 1.0, 0.0).astype(BF16)


def split_kernel(field, out, rows):
    rows[...] = dot(field[...], spread_rows(256, 256))
    for z in range(2):
        for x in range(4):
            col = z * PLANE + x * 256
            for e in range(8):
                line = z * 32 + e * 4 + x
                out[e : e + 1, col : col + 256] = rows[line : line + 1, :]


def activate_kernel(
    near, across, weight, bias, cot, turned, active, share, dpre, moved, taps, cols
):
    hidden = jnp.concatenate([near[...], across[...]], axis=0)
    taps[...] = dot(weight[...], hidden)

    def column(plane, x, parity):
        return plane * PLANE + (x % 4) * 256 + parity * LANE

    for z in range(2):
        for x in range(4):
            for parity in range(2):
                pre = bias[...]
                for ty in (-1, 0, 1):
                    other = (parity + ty) % 2
                    step = (parity + ty) // 2
                    part = None
                    for tz in range(3):
                        for tx in range(3):
                            row = (tz * 9 + tx * 3 + ty + 1) * 8
                            col = column(z + tz, x + tx - 1, other)
                            term = taps[row : row + 8, col : col + LANE]
                            part = term if part is None else part + term
                    pre = pre + ahead(part, step)
                sigma = 1.0 / (1.0 + jnp.exp(-pre))
                col = column(z, x, parity)
                active[:, col : col + LANE] = pre * sigma
                slope = cot[:, col : col + LANE] * sigma * (1.0 + pre * (1.0 - sigma))
                dpre[:, col : col + LANE] = slope.astype(BF16).astype(F32)

    for z in range(2):
        cols[z * LANE + 72 : (z + 1) * LANE, :] = jnp.zeros((LANE - 72, PLANE), F32)
        for x in range(4):
            for parity in range(2):
                for ty in (-1, 0, 1):
                    other = (parity - ty) % 2
                    step = (parity - ty) // 2
                    for tx in range(3):
                        col = column(z, x - (tx - 1), other)
                        value = ahead(dpre[:, col : col + LANE], step)
                        row = z * LANE + (tx * 3 + ty + 1) * 8
                        col = column(0, x, parity)
                        cols[row : row + 8, col : col + LANE] = value
    moved[...] = cols[...].astype(BF16)
    channel_sums(turned, moved, slice(64, 128), share)


def channel_sums(turned, moved, rows, out):
    out[:, :PLANE] = dot(turned[rows, 2 * LANE :], moved[:LANE]).astype(BF16)
    out[:, PLANE : 2 * PLANE] = dot(turned[rows, LANE:], moved[...]).astype(BF16)
    out[:, 2 * PLANE : 3 * PLANE] = dot(turned[rows, : 2 * LANE], moved[...]).astype(BF16)
    out[:, 3 * PLANE :] = dot(turned[rows, :LANE], moved[LANE:]).astype(BF16)


def result_kernel(active, result, rows):
    for z in range(2):
        for x in range(4):
            col = z * PLANE + x * 256
            both = active[:, col : col + 256].astype(BF16)
            natural = dot(both, spread_rows(256, 256), ((1,), (1,)))
            for e in range(8):
                line = z * 32 + e * 4 + x
                rows[line : line + 1, :] = natural[e : e + 1, :]
    for z in range(2):
        for e in range(8):
            line = z * 32 + e * 4
            result[z, e] = rows[line : line + 4, :].astype(BF16)


def mix_back_kernel(near, across, turned, dpre, moved, own, raw):
    channel_sums(turned, moved, slice(0, 64), own)
    for tz in range(3):
        for block, columns in ((near, slice(0, 64)), (across, slice(64, 128))):
            one = dot(moved[:LANE], block[:, tz * PLANE : (tz + 1) * PLANE], ((1,), (1,)))
            two = dot(moved[LANE:], block[:, (tz + 1) * PLANE : (tz + 2) * PLANE], ((1,), (1,)))
            raw[tz * 72 : (tz + 1) * 72, columns] = (one + two)[:72]
    total = jnp.sum(dpre[...], axis=1, keepdims=True)
    raw[216:224, :] = jnp.broadcast_to(total, (8, LANE))
    raw[224:256, :] = jnp.zeros((32, LANE), F32)


def pick_columns(field, out, base):
    for kx in range(4):
        for ky in range(4):
            parity, step = (ky - 1) % 2, (ky - 1) // 2
            for xi in range(2):
                x = (2 * xi - 1 + kx) % 4
                col = x * 256 + parity * LANE
                row = base + (kx * 4 + ky) * 8
                out[row : row + 8, xi * LANE : (xi + 1) * LANE] = ahead(
                    field[:, col : col + LANE], step
                )


def lift_back_kernel(parts, source, raw_second, low, high, message, cols, raw, second):
    total = parts[0].astype(F32)
    for f in range(1, parts.shape[0]):
        total = total + parts[f].astype(F32)
    low[...] = total[:, : 2 * PLANE].astype(BF16)
    high[...] = total[:, 2 * PLANE :].astype(BF16)
    for plane in range(4):
        pick_columns(total[:, plane * PLANE : (plane + 1) * PLANE], cols, plane * LANE)
    pairs = (((0, 1), (2, 2)), ((1, 1), (3, 2)), ((0, 0), (2, 1)), ((1, 0), (3, 1)))
    for kz, met in enumerate(pairs):
        part = None
        for plane, place in met:
            term = dot(
                cols[plane * LANE : (plane + 1) * LANE, :].astype(BF16),
                source[:, place * 256 : (place + 1) * 256],
                ((1,), (1,)),
            )
            part = term if part is None else part + term
        raw[kz * LANE : (kz + 1) * LANE, :] = part
    second[...] = raw_second[...]
    sums = (second[216:224, :], jnp.broadcast_to(jnp.sum(total, axis=1, keepdims=True), (8, LANE)))
    for i, value in enumerate(sums):
        high = value.astype(BF16).astype(F32)
        second[216 + 16 * i : 224 + 16 * i, :] = high
        second[224 + 16 * i : 232 + 16 * i, :] = value - high
    for i in range(NEAR):
        block = raw[64 * i : 64 * (i + 1), :].astype(BF16)
        message[i, 0:64, :] = block[:, :LANE]
        message[i, 64:128, :] = block[:, LANE:]
        message[i, 128:160, :] = second[32 * i : 32 * (i + 1), :].astype(BF16)


def lift_input_kernel(low, low_other, high, high_other, weight, share, cols):
    for half, (one, other) in enumerate(((low, low_other), (high, high_other))):
        total = (one[...].astype(F32) + other[...].astype(F32)).astype(BF16).astype(F32)
        pick_columns(total[:, :PLANE], cols, 2 * half * LANE)
        pick_columns(total[:, PLANE:], cols, (2 * half + 1) * LANE)
    share[...] = dot(weight[...], cols[...].astype(BF16)).astype(BF16)


def sum_kernel(parts, out):
    total = parts[0].astype(F32)
    for i in range(1, parts.shape[0]):
        total = total + parts[i].astype(F32)
    out[...] = total.astype(out.dtype)


def plane_kernel(parts, out):
    total = parts[0].astype(F32)
    for i in range(1, parts.shape[0]):
        total = total + parts[i].astype(F32)
    out[:, 0, :] = total[:, :LANE].astype(BF16)
    out[:, 1, :] = total[:, LANE:].astype(BF16)


def pair_kernel(one, other, out):
    total = (one[...].astype(F32) + other[...].astype(F32)).astype(BF16)
    out[...] = jnp.broadcast_to(total, out.shape)


def as_row(column):
    here = lax.broadcasted_iota(jnp.int32, (8, LANE), 0)
    lane = lax.broadcasted_iota(jnp.int32, (8, LANE), 1)
    return jnp.sum(jnp.where(here == lane, column, 0.0), axis=0, keepdims=True)[:, :8]


def finish_kernel(scale, parts, order, first, second, first_bias, second_bias, left, right, rest):
    for i in range(NEAR):
        left[64 * i : 64 * (i + 1), :] = parts[i, 0:64, :].astype(F32) * scale
        right[64 * i : 64 * (i + 1), :] = parts[i, 64:128, :].astype(F32) * scale
        rest[32 * i : 32 * (i + 1), :] = parts[i, 128:160, :].astype(F32)
    for d in range(8):
        first[d, :, :LANE] = left[pl.ds(d, 64, stride=8), :]
        first[d, :, LANE:] = right[pl.ds(d, 64, stride=8), :]
    second[...] = dot(rest[...].astype(BF16), order[...])[0:216] * scale
    second_bias[...] = as_row(rest[216:224, :] + rest[224:232, :]) * scale
    first_bias[...] = as_row(rest[232:240, :] + rest[240:248, :]) * scale


def shifted(value, step):
    count = lax.axis_size("space")
    return lax.ppermute(value, "space", [(i, (i + step) % count) for i in range(count)])


def chip_exchange(value):
    count = lax.axis_size("filt")
    groups = [list(range(core, count, 2)) for core in range(2)]
    return lax.all_to_all(value, "filt", 0, 0, axis_index_groups=groups, tiled=True)


def other_core(value):
    count = lax.axis_size("filt")
    return lax.ppermute(value, "filt", [(i, i ^ 1) for i in range(count)])


def pair_gather(copies):
    slabs, blocks = lax.axis_size("space"), lax.axis_size("filt")
    groups = [
        [s * blocks + f for s in (low, low + 1) for f in range(blocks)] for low in range(0, slabs, 2)
    ]
    return lax.all_to_all(copies, ("space", "filt"), 0, 0, axis_index_groups=groups, tiled=True)


def outer_plane(value):
    count = lax.axis_size("space")
    pairs = [(i, (((i + 1) ^ 1) - 1) % count) for i in range(count)]
    return lax.ppermute(value, "space", pairs)


def by_core(weight, core):
    split = weight.reshape(weight.shape[:-1] + (8, 2, 8))
    split = jnp.where(core == 0, split, jnp.flip(split, -2))
    return jnp.swapaxes(split, -3, -2).reshape(weight.shape)


def partner(value, turn):
    slabs, blocks = lax.axis_size("space"), lax.axis_size("filt")
    groups = slabs // NEAR
    pairs = []
    for s in range(slabs):
        for f in range(blocks):
            ends = (turn + f) % 2
            other = (((s // NEAR + ends) ^ 1) - ends) % groups * NEAR + s % NEAR
            pairs.append((s * blocks + f, other * blocks + f))
    return lax.ppermute(value, ("space", "filt"), pairs)


def near_exchange(value):
    count = lax.axis_size("space")
    groups = [[g + i for i in range(NEAR)] for g in range(0, count, NEAR)]
    return lax.all_to_all(value, "space", 0, 0, axis_index_groups=groups, tiled=True)


def per_device(volume, first_weight, first_bias, second_weight, second_bias, cotangent):
    struct = jax.ShapeDtypeStruct
    wide = lambda bias: jnp.broadcast_to(bias.astype(F32)[:, None], (8, LANE))
    core = lax.axis_index("filt") % 2
    odd = lax.axis_index("space") % 2
    copies = vmem_call(
        copies_kernel,
        struct((32, 16, 256), BF16),
        [pltpu.VMEM((16, 2, LANE), BF16)],
        [pl.BlockSpec(memory_space=pl.ANY)],
        60 * 1024 * 1024,
    )(volume.reshape(16, 2, LANE))
    pair = pair_gather(copies).reshape(2, 256, 256)
    given = (first_weight, wide(first_bias), second_weight, wide(second_bias), cotangent)
    pair, given = lax.optimization_barrier((pair, given))
    first_weight, first_wide, second_weight, second_wide, cotangent = given
    first_rows = first_weight.transpose(1, 0, 2).reshape(512, 256)
    first_turned = first_weight.transpose(2, 1, 0).reshape(256, 512)
    second = by_core(second_weight, core)
    second_rows = second.transpose(1, 0, 2).reshape(216, LANE)
    second_rows = jnp.pad(second_rows, ((0, 8), (0, 0)))
    second_turned = second.transpose(2, 1, 0).reshape(LANE, 3, 72)[:, ::-1]
    second_turned = jnp.pad(second_turned, ((0, 0), (0, 0), (0, 56))).reshape(LANE, 384)
    order = by_core(jnp.eye(LANE, dtype=BF16), core).T
    cot = vmem_call(
        split_kernel, struct((8, 2 * PLANE), F32), [pltpu.VMEM((64, 256), F32)]
    )(cotangent.reshape(64, 256))
    outer = outer_plane(lax.dynamic_index_in_dim(pair, odd, 0, keepdims=False))
    ready = (first_rows, first_turned, second_rows, second_turned, order, cot)
    outer, ready = lax.optimization_barrier((outer, ready))
    first_rows, first_turned, second_rows, second_turned, order, cot = ready
    whole = pl.BlockSpec(memory_space=pltpu.VMEM)
    source, hidden = vmem_call(
        hidden_kernel,
        (struct((256, 768), BF16), struct((8, 8, 4 * PLANE), BF16)),
        [pltpu.VMEM((512, 768), F32)],
        [pl.BlockSpec(memory_space=pltpu.SMEM)] + [whole] * 4,
    )(odd.reshape(1), first_rows, pair.reshape(512, 256), outer, first_wide)
    hidden = chip_exchange(hidden).reshape(64, 4 * PLANE)

    across = other_core(hidden)
    active, share, dpre, moved = vmem_call(
        activate_kernel,
        (
            struct((8, 2 * PLANE), F32),
            struct((64, 4 * PLANE), BF16),
            struct((8, 2 * PLANE), F32),
            struct((256, PLANE), BF16),
        ),
        [pltpu.VMEM((224, 4 * PLANE), F32), pltpu.VMEM((256, PLANE), F32)],
    )(hidden, across, second_rows, second_wide, cot, second_turned)
    own, raw_second = vmem_call(
        mix_back_kernel, (struct((64, 4 * PLANE), BF16), struct((256, LANE), F32))
    )(hidden, across, second_turned, dpre, moved)
    share = vmem_call(pair_kernel, struct((64, 4 * PLANE), BF16))(own, other_core(share))
    parts = chip_exchange(share.reshape(8, 8, 4 * PLANE))

    low, high, message = vmem_call(
        lift_back_kernel,
        (
            struct((8, 2 * PLANE), BF16),
            struct((8, 2 * PLANE), BF16),
            struct((NEAR, 160, LANE), BF16),
        ),
        [pltpu.VMEM((512, 256), F32), pltpu.VMEM((512, 256), F32), pltpu.VMEM((256, LANE), F32)],
    )(parts, source, raw_second)

    low_other = shifted(high, 1)
    high_other = shifted(low, -1)
    message = near_exchange(message)
    result = vmem_call(
        result_kernel, struct((2, 8, 4, 256), BF16), [pltpu.VMEM((64, 256), F32)]
    )(active)
    message, low_other, high_other, result = lax.optimization_barrier(
        (message, low_other, high_other, result)
    )
    share = vmem_call(
        lift_input_kernel, struct((256, 256), BF16), [pltpu.VMEM((512, 256), F32)]
    )(low, low_other, high, high_other, first_turned)
    mine = vmem_call(sum_kernel, struct((160, LANE), BF16))(message)
    share, mine = lax.optimization_barrier((share, mine))
    other = partner(mine, 0)
    share = lax.all_to_all(share.reshape(16, 16, 256), "filt", 0, 0, tiled=True)
    other, share = lax.optimization_barrier((other, share))
    mine = vmem_call(pair_kernel, struct((160, LANE), BF16))(mine, other)
    other = partner(mine, 1)
    grad_volume = vmem_call(plane_kernel, struct((16, 2, LANE), BF16))(share)
    other, grad_volume = lax.optimization_barrier((other, grad_volume))
    message = vmem_call(pair_kernel, struct((NEAR, 160, LANE), BF16))(mine, other)
    message = near_exchange(message)

    total_cells = volume.shape[0] * lax.axis_size("space") * 8 * volume.shape[2] * volume.shape[3]
    scale = 1.0 / math.sqrt(total_cells)
    first, second, sum_first, sum_second = vmem_call(
        lambda *refs: finish_kernel(scale, *refs),
        (
            struct((8, 64, 256), F32),
            struct((216, LANE), F32),
            struct((1, 8), F32),
            struct((1, 8), F32),
        ),
        [pltpu.VMEM((520, LANE), F32), pltpu.VMEM((520, LANE), F32), pltpu.VMEM((256, LANE), F32)],
    )(message, order)
    return (
        result,
        grad_volume.reshape(1, 16, 2, 128),
        first,
        sum_first.reshape(8),
        second.reshape(27, 8, LANE).transpose(1, 0, 2),
        sum_second.reshape(8),
    )


def solution(mesh):
    placed = (
        P("space", "filt", None, None),
        P("filt", None, None),
        P("filt"),
        P("filt", None, None),
        P("filt"),
        P("space", "filt", None, None),
    )
    return jax.shard_map(
        per_device,
        mesh=mesh,
        in_specs=placed,
        out_specs=(
            P("space", "filt", None, None),
            P("space", "filt", None, None),
            P("filt", None, None),
            P("filt"),
            P("filt", None, None),
            P("filt"),
        ),
        check_vma=False,
    )
```
